32 devices in a mesh: groups: 2 (over x), clus: 16 (over z, y, core).
Axes of the slice: x: 2, y: 2, z: 4, core: 2. Of those that a mesh axis runs over, the one named last changes fastest.
Arguments:
- tokens: bfloat16 [10240, 4096], P(('groups', 'clus')), parts along dimension 0, may hold values from -6 to 6
- proj_weight: bfloat16 [4096, 1024], replicated, may hold values from -0.09375 to 0.09375
- labels: int32 [10240, 1], P(('groups', 'clus')), parts along dimension 0, may hold values from 0 to 15; in each aligned block of 320 rows (0 to 319, 320 to 639, ...) at most 40 rows name the same one
- valid_rows: int32 [10240], P(('groups', 'clus')), parts along dimension 0, may hold values 0 or 1
Outputs:
- similar: float32 [32, 640, 640], P(('groups', 'clus')), parts along dimension 0
- nearest: float32 [10240], P(('groups', 'clus')), parts along dimension 0
- centre_dist: float32 [10240], P(('groups', 'clus')), parts along dimension 0
The draws below stay inside these ranges and needn't reach their ends.
There are 2 independent parts, one for each index of `groups`. The reference program is written for one: setup_inputs(seed, part) draws one part's arguments, and reference() takes and returns one part's arrays. A program takes and returns all parts, laid end to end along the dimension named above; an argument that names none is the same for every part. Nothing has to cross between parts.
Inputs may be any that keep to these rules, and one draw needn't show every extreme that they name: `labels`: within each device's block of 320 rows no cluster is named by more than 40 rows, and some cluster reaches 40 in some block; every cluster is named somewhere.
All inputs are finite; a program needn't handle non-finite values. No bound on the sum of `valid_rows` on one device may be relied on, other than what follows from the above.
Results may differ from the reference program's by a relative error of at most 0.002.
Values may be sent and summed in bfloat16 or wider, within the bound.
No kernel may reach another device: no remote copies, remote signals or barrier semaphores. Data moves between devices by JAX's collectives and lax.ppermute only.
A program may use at most 64 MiB of HBM per device.

```python
import math
import jax
import jax.numpy as jnp
import numpy as np
from jax import lax

D = 4096
E = 1024
ROW_DEV = 320
ROWS = 5120
CLUSTERS = 16
SLOT = 40
N_CLUS = 16


def plant(values, key, low, largest):
    index_at = [jax.random.randint(jax.random.fold_in(key, axis), (), 0, length) for axis, length in enumerate(values.shape)]
    longest = values.shape.index(max(values.shape))
    next_to = index_at[:longest] + [(index_at[longest] + 1) % values.shape[longest]] + index_at[longest + 1:]
    return values.at[tuple(index_at)].set(low).at[tuple(next_to)].set(largest)


def levels(rng, dims, split, smallest, high):
    def one(position, shards_of):
        heights = jax.random.uniform(jax.random.fold_in(jax.random.fold_in(rng, 6), position), (shards_of,), jnp.float32, smallest / len(split), high / len(split))
        return jnp.repeat(jnp.exp(heights), dims[position] // shards_of).reshape((-1,) + (1,) * (len(dims) - position - 1))

    level = one(*split[0])
    for cut in split[1:]:
        level = level * one(*cut)
    return level


def assign_block(stream_key, own, number, rows, number_of, top, reach, lean):
    ranking = jax.random.permutation(stream_key, number_of)
    packed, usual = portions_of(number_of, rows * top, reach, lean, True), portions_of(number_of, rows * top, reach, lean, False)
    places = jnp.arange(number_of)

    def named(sizes, turn):
        used = int((sizes > 0).sum())
        fixed = max(1, used // 4)
        shifted = fixed + (places - fixed + turn * (used - fixed)) % max(1, number_of - fixed)
        return jnp.zeros((number_of,), jnp.int32).at[ranking[jnp.where(places < fixed, places, shifted)]].set(jnp.asarray(sizes, jnp.int32))

    sizes = jnp.where(number % 4 == 0, named(packed, number // 4), named(usual, number - number // 4 - 1))
    mixed = jax.random.permutation(jax.random.fold_in(own, 3), number_of)
    donor, sink = mixed[0:number_of // 2 * 2:2], mixed[1:number_of // 2 * 2:2]
    margin = jnp.minimum(sizes[donor] - 1, reach - sizes[sink]) // 2
    margin = jnp.where((donor == ranking[0]) | (sink == ranking[0]) | (sizes[sink] == 0), 0, jnp.maximum(margin, 0))
    shifted = jax.random.randint(jax.random.fold_in(own, 4), (number_of // 2,), 0, 1 << 20) % (margin + 1)
    sizes = sizes.at[donor].add(-shifted).at[sink].add(shifted)
    items = jnp.searchsorted(jnp.cumsum(sizes), jnp.arange(rows * top), side="right").astype(jnp.int32)
    table = items.reshape(top, rows).T
    table = table[jax.random.permutation(jax.random.fold_in(own, 1), rows)]
    turn = jax.random.randint(jax.random.fold_in(own, 2), (rows, 1), 0, top)
    return jnp.take_along_axis(table, (jnp.arange(top)[None, :] + turn) % top, axis=1)


def portions_of(number_of, total, bound, lean, full):
    portions = [(1 << 20) // math.isqrt(standing ** lean) + 1 for standing in range(1, number_of + 1)]
    largest = bound if full else min(bound, max(-(-total // number_of), total * portions[0] // sum(portions)))
    least = 1 if total - largest >= number_of - 1 else 0
    counts, surplus = [largest] + [least] * (number_of - 1), total - largest - least * (number_of - 1)
    while surplus > 0:
        free = [i for i in range(1, number_of) if counts[i] < largest] or [i for i in range(1, number_of) if counts[i] < bound]
        mass, remaining = sum([portions[i] for i in free]), surplus
        for i in free:
            extra = min(bound - counts[i], max(1, remaining * portions[i] // mass), surplus)
            counts[i] = counts[i] + extra
            surplus = surplus - extra
    return np.array(counts)


def noise(key, extent, spread, most, shards=(), held_as=jnp.bfloat16):
    array = jax.random.normal(key, extent, jnp.float32) * spread
    if len(shards) > 0:
        array = levels(key, extent, shards, -0.22, 0.18) * array
    return jnp.clip(array, min=-most, max=most).astype(held_as)


def setup_inputs(seed: int = 0, part: int = 0) -> dict:
    key_of = jax.random.split(jax.random.key(seed), 5)
    own_keys = jax.random.split(jax.random.fold_in(key_of[4], part), 5)
    tokens = noise(own_keys[0], (ROWS, D), 1.0, 6.0, ((0, 16),))
    proj_weight = noise(key_of[1], (D, E), D ** -0.5, 0.09375)
    labels_keys = jax.random.split(jax.random.fold_in(own_keys[2], 1), ROWS // ROW_DEV)
    labels_turns = jax.random.permutation(jax.random.fold_in(own_keys[2], 3), ROWS // ROW_DEV)
    labels = jax.vmap(lambda own, number: assign_block(jax.random.fold_in(own_keys[2], 2), own, number, ROW_DEV, CLUSTERS, 1, SLOT, 2))(labels_keys, labels_turns).reshape((ROWS, 1))
    valid_rows = plant((jax.random.randint(own_keys[3], (ROWS,), 0, 8) < 7).astype(jnp.int32), jax.random.fold_in(own_keys[3], 1), 0, 1)
    return {"tokens": tokens, "proj_weight": proj_weight, "labels": labels, "valid_rows": valid_rows}


def reference(tokens, proj_weight, labels, valid_rows):
    embed = jnp.dot(tokens, proj_weight, preferred_element_type=jnp.float32)
    mask_float = valid_rows.astype(jnp.float32)
    scale = lax.rsqrt(lax.optimization_barrier(jnp.sum(embed * embed, axis=1)) + 1e-06)
    unit = (embed * (scale * mask_float)[:, None]).astype(jnp.bfloat16)
    label_flat = labels[:, 0]
    onehot = (label_flat[:, None] == jnp.arange(CLUSTERS, dtype=jnp.int32)[None, :]).astype(jnp.int32)
    blocked = onehot.reshape(N_CLUS, ROW_DEV, CLUSTERS)
    counted = jnp.cumsum(blocked, axis=1).reshape(ROWS, CLUSTERS)
    rank_inside = lax.optimization_barrier(jnp.sum((counted - 1) * onehot, axis=1)).astype(jnp.int32)
    block_index = (jnp.arange(ROWS, dtype=jnp.int32) // ROW_DEV).astype(jnp.int32)
    slot_index = (block_index * SLOT + rank_inside).astype(jnp.int32)
    width_all = N_CLUS * SLOT
    members = jnp.zeros((CLUSTERS, width_all, E), jnp.bfloat16).at[label_flat, slot_index].set(unit)
    itself = jnp.eye(width_all, dtype=jnp.bool_)

    def per_cluster(member_rows):
        ones_row = jnp.ones((1, width_all), jnp.bfloat16)
        centroid_sum = jnp.dot(ones_row, member_rows, preferred_element_type=jnp.float32)[0]
        centroid_unit = centroid_sum * lax.rsqrt(jnp.sum(centroid_sum * centroid_sum) + 1e-06)
        gram_tile = lax.dot_general(member_rows, member_rows, (((1,), (1,)), ((), ())), preferred_element_type=jnp.float32)
        slot_near = lax.optimization_barrier(jnp.max(jnp.where(itself, 0.0, gram_tile), axis=1))
        slot_dist = 1.0 - lax.optimization_barrier(jnp.sum(member_rows * centroid_unit[None, :], axis=1))
        return (gram_tile, slot_near, slot_dist)
    similar, slot_near, slot_dist = lax.map(per_cluster, members)
    nearest = slot_near[label_flat, slot_index] * mask_float
    centre_dist = slot_dist[label_flat, slot_index] * mask_float
    return (similar, nearest, centre_dist)
```

```python
import functools

import jax
import jax.numpy as jnp
from jax import lax
from jax.experimental import pallas as pl
from jax.experimental.pallas import tpu as pltpu
from jax.sharding import PartitionSpec as P

F32 = jnp.float32
BF16 = jnp.bfloat16
VMEM_BYTES = 48 * 1024 * 1024


def split3(x):
    hi = x.astype(BF16)
    rest = x - hi.astype(F32)
    mid = rest.astype(BF16)
    low = (rest - mid.astype(F32)).astype(BF16)
    return hi, mid, low


def embed_kernel(slot_count, steps, tokens_ref, weight_ref, label_ref, valid_ref, packed_ref, rank_ref, total, place):
    step = pl.program_id(0)
    rows = total.shape[0]
    width_all = place.shape[0]
    part = jnp.dot(tokens_ref[...], weight_ref[...], preferred_element_type=F32)

    @pl.when(step == 0)
    def _():
        total[...] = part
        label_row = label_ref[...].astype(F32)
        below = lax.broadcasted_iota(jnp.int32, (rows, rows), 0)
        across = lax.broadcasted_iota(jnp.int32, (rows, rows), 1)
        label_col = jnp.sum(jnp.where(below == across, label_row, 0.0), axis=1, keepdims=True)
        earlier = (label_col == label_row) & (below < across)
        rank = jnp.sum(jnp.where(earlier, 1.0, 0.0), axis=0, keepdims=True).astype(jnp.int32)
        rank_ref[...] = rank
        slot = label_ref[...] * slot_count + rank
        slot = jnp.where(valid_ref[...] > 0, slot, -1)
        slots = lax.broadcasted_iota(jnp.int32, (width_all, rows), 0)
        place[...] = jnp.where(slots == slot, 1.0, 0.0).astype(BF16)

    @pl.when(step > 0)
    def _():
        total[...] += part

    @pl.when(step == steps - 1)
    def _():
        embed = total[...]
        scale = lax.rsqrt(jnp.sum(embed * embed, axis=1, keepdims=True) + 1e-06)
        unit = (embed * scale).astype(BF16)
        packed_ref[...] = jnp.dot(place[...], unit, preferred_element_type=F32).astype(BF16)


def embed_and_pack(tokens, weight, label_row, valid_row, owners, slot_count):
    rows, depth = tokens.shape
    width = weight.shape[1]
    steps = 8 if depth % 1024 == 0 else 1
    block = depth // steps
    width_all = owners * slot_count
    return pl.pallas_call(
        functools.partial(embed_kernel, slot_count, steps),
        grid=(steps,),
        in_specs=[
            pl.BlockSpec((rows, block), lambda k: (0, k)),
            pl.BlockSpec((block, width), lambda k: (k, 0)),
            pl.BlockSpec((1, rows), lambda k: (0, 0)),
            pl.BlockSpec((1, rows), lambda k: (0, 0)),
        ],
        out_specs=(
            pl.BlockSpec((width_all, width), lambda k: (0, 0)),
            pl.BlockSpec((1, rows), lambda k: (0, 0)),
        ),
        out_shape=(
            jax.ShapeDtypeStruct((width_all, width), BF16),
            jax.ShapeDtypeStruct((1, rows), jnp.int32),
        ),
        scratch_shapes=[pltpu.VMEM((rows, width), F32), pltpu.VMEM((width_all, rows), BF16)],
        compiler_params=pltpu.CompilerParams(vmem_limit_bytes=VMEM_BYTES),
        cost_estimate=pl.CostEstimate(
            flops=2 * rows * depth * width, bytes_accessed=2 * depth * width + 2 * rows * depth, transcendentals=0
        ),
    )(tokens, weight, label_row, valid_row)


def score_kernel(slot_count, half, members_ref, message_ref, near_col, sum_col):
    width_all = members_ref.shape[0]
    owners, lanes = message_ref.shape
    block = 128
    for b in range(width_all // block):
        gram = lax.dot_general(
            members_ref[b * block:(b + 1) * block, :], members_ref[...], (((1,), (1,)), ((), ())), preferred_element_type=F32
        )
        own = lax.broadcasted_iota(jnp.int32, (block, width_all), 0) + b * block
        other = lax.broadcasted_iota(jnp.int32, (block, width_all), 1)
        near_col[b * block:(b + 1) * block, :] = jnp.max(jnp.where(own == other, 0.0, gram), axis=1, keepdims=True)
        sum_col[b * block:(b + 1) * block, :] = jnp.sum(gram, axis=1, keepdims=True)
    square = jnp.maximum(jnp.sum(sum_col[...], axis=0, keepdims=True), 0.0)
    dist = 1.0 - sum_col[...] * lax.rsqrt(square + 1e-06)
    slot = lax.broadcasted_iota(jnp.int32, (width_all, lanes), 0)
    within = slot - (slot // slot_count) * slot_count
    lane = lax.broadcasted_iota(jnp.int32, (width_all, lanes), 1)
    spread = jnp.where(lane == within, near_col[...], jnp.where(lane == within + half, dist, 0.0))
    source = lax.broadcasted_iota(jnp.int32, (owners, width_all), 0) * slot_count
    member = lax.broadcasted_iota(jnp.int32, (owners, width_all), 1)
    chosen = jnp.where((member >= source) & (member < source + slot_count), 1.0, 0.0).astype(BF16)
    out = jnp.zeros((owners, lanes), F32)
    for piece in split3(spread):
        out += jnp.dot(chosen, piece, preferred_element_type=F32)
    message_ref[...] = out


def scores(members, owners, slot_count, half):
    width_all = members.shape[0]
    return pl.pallas_call(
        functools.partial(score_kernel, slot_count, half),
        out_shape=jax.ShapeDtypeStruct((owners, 2 * half), F32),
        scratch_shapes=[pltpu.VMEM((width_all, 1), F32)] * 2,
        compiler_params=pltpu.CompilerParams(vmem_limit_bytes=VMEM_BYTES),
    )(members)


def gram_kernel(members_ref, gram_ref):
    width_all = members_ref.shape[0]
    block = 128
    here = pl.program_id(0) * block
    gram_ref[0] = lax.dot_general(
        members_ref[pl.ds(pl.multiple_of(here, block), block), :],
        members_ref[...],
        (((1,), (1,)), ((), ())),
        preferred_element_type=F32,
    )


def gram(members):
    width_all, width = members.shape
    block = 128
    return pl.pallas_call(
        gram_kernel,
        grid=(width_all // block,),
        in_specs=[pl.BlockSpec((width_all, width), lambda b: (0, 0))],
        out_specs=pl.BlockSpec((1, block, width_all), lambda b: (0, b, 0)),
        out_shape=jax.ShapeDtypeStruct((1, width_all, width_all), F32),
        compiler_params=pltpu.CompilerParams(vmem_limit_bytes=VMEM_BYTES),
        cost_estimate=pl.CostEstimate(
            flops=2 * width_all * width_all * width,
            bytes_accessed=2 * width_all * width + 4 * width_all * width_all,
            transcendentals=0,
        ),
    )(members)


def fetch_kernel(half, message_ref, label_ref, rank_ref, valid_ref, near_ref, dist_ref):
    owners, lanes = message_ref.shape
    rows = label_ref.shape[1]
    owner = lax.broadcasted_iota(jnp.int32, (owners, rows), 0)
    chosen = jnp.where(owner == label_ref[...], 1.0, 0.0).astype(BF16)
    mine = jnp.zeros((lanes, rows), F32)
    for piece in split3(message_ref[...]):
        mine += lax.dot_general(piece, chosen, (((0,), (0,)), ((), ())), preferred_element_type=F32)
    lane = lax.broadcasted_iota(jnp.int32, (lanes, rows), 0)
    rank = rank_ref[...]
    valid = valid_ref[...].astype(F32)
    near_ref[...] = jnp.sum(jnp.where(lane == rank, mine, 0.0), axis=0, keepdims=True) * valid
    dist_ref[...] = jnp.sum(jnp.where(lane == rank + half, mine, 0.0), axis=0, keepdims=True) * valid


def fetch(message, label_row, rank_row, valid_row, half):
    rows = label_row.shape[1]
    return pl.pallas_call(
        functools.partial(fetch_kernel, half),
        out_shape=(jax.ShapeDtypeStruct((1, rows), F32),) * 2,
    )(message, label_row, rank_row, valid_row)


def per_device(tokens, proj_weight, labels, valid_rows):
    row_count = tokens.shape[0]
    owners = lax.axis_size("clus")
    slot_count = 2 * row_count // owners
    width_all = owners * slot_count
    half = -(-slot_count // 64) * 64
    label_row = labels.reshape(1, row_count)
    valid_row = valid_rows.reshape(1, row_count)
    packed, rank_row = embed_and_pack(tokens, proj_weight, label_row, valid_row, owners, slot_count)
    arrived = lax.all_to_all(
        packed.reshape(owners, slot_count, -1), "clus", split_axis=0, concat_axis=0, tiled=True
    )
    members = arrived.reshape(width_all, -1)
    message = scores(members, owners, slot_count, half)
    returned = lax.all_to_all(message, "clus", split_axis=0, concat_axis=0, tiled=True)
    similar = gram(members)
    nearest, centre_dist = fetch(returned, label_row, rank_row, valid_row, half)
    return (similar, nearest.reshape(row_count), centre_dist.reshape(row_count))


def solution(mesh):
    return jax.shard_map(
        per_device,
        mesh=mesh,
        in_specs=(
            P(("groups", "clus"), None),
            P(),
            P(("groups", "clus"), None),
            P(("groups", "clus")),
        ),
        out_specs=(P(("groups", "clus"), None, None), P(("groups", "clus")), P(("groups", "clus"))),
        check_vma=False,
    )
```

```python
import functools

import jax
import jax.numpy as jnp
from jax import lax
from jax.experimental import pallas as pl
from jax.experimental.pallas import tpu as pltpu
from jax.sharding import PartitionSpec as P

F32 = jnp.float32
BF16 = jnp.bfloat16
VMEM_BYTES = 48 * 1024 * 1024
EMBED_VMEM_BYTES = 60 * 1024 * 1024


def split3(x):
    hi = x.astype(BF16)
    rest = x - hi.astype(F32)
    mid = rest.astype(BF16)
    low = (rest - mid.astype(F32)).astype(BF16)
    return hi, mid, low


def place_rows(label_row, valid_row, slot_count, width_all):
    rows = label_row.shape[1]
    label = label_row.astype(F32)
    below = lax.broadcasted_iota(jnp.int32, (rows, rows), 0)
    across = lax.broadcasted_iota(jnp.int32, (rows, rows), 1)
    label_col = jnp.sum(jnp.where(below == across, label, 0.0), axis=1, keepdims=True)
    earlier = (label_col == label) & (below < across)
    rank = jnp.sum(jnp.where(earlier, 1.0, 0.0), axis=0, keepdims=True).astype(jnp.int32)
    slot = jnp.where(valid_row > 0, label_row * slot_count + rank, -1)
    slots = lax.broadcasted_iota(jnp.int32, (width_all, rows), 0)
    return rank, jnp.where(slots == slot, 1.0, 0.0).astype(BF16)


def embed_kernel(
    slot_count, tokens_hbm, weight_hbm, label_hbm, valid_hbm, packed_ref, rank_ref,
    tokens, weight, total, place, label_ref, valid_ref, token_sem, weight_sem, small_sem,
):
    steps = token_sem.shape[0]
    block = tokens.shape[1] // steps
    small = (
        pltpu.make_async_copy(label_hbm, label_ref, small_sem.at[0]),
        pltpu.make_async_copy(valid_hbm, valid_ref, small_sem.at[1]),
    )
    for copy in small:
        copy.start()
    copies = []
    for k in range(steps):
        part = slice(k * block, (k + 1) * block)
        pair = (
            pltpu.make_async_copy(tokens_hbm.at[:, part], tokens.at[:, part], token_sem.at[k]),
            pltpu.make_async_copy(weight_hbm.at[part, :], weight.at[part, :], weight_sem.at[k]),
        )
        for copy in pair:
            copy.start()
        copies.append(pair)
    for copy in small:
        copy.wait()
    rank, chosen = place_rows(label_ref[...], valid_ref[...].reshape(label_ref.shape), slot_count, place.shape[0])
    rank_ref[...] = rank
    place[...] = chosen
    for k, pair in enumerate(copies):
        for copy in pair:
            copy.wait()
        part = slice(k * block, (k + 1) * block)
        product = jnp.dot(tokens[:, part], weight[part, :], preferred_element_type=F32)
        if k == 0:
            total[...] = product
        else:
            total[...] += product
    embed = total[...]
    scale = lax.rsqrt(jnp.sum(embed * embed, axis=1, keepdims=True) + 1e-06)
    unit = (embed * scale).astype(BF16)
    packed_ref[...] = jnp.dot(place[...], unit, preferred_element_type=F32).astype(BF16)


def embed_and_pack(tokens, weight, label_row, valid, owners, slot_count):
    rows, depth = tokens.shape
    width = weight.shape[1]
    steps = 8 if depth % 1024 == 0 else 1
    width_all = owners * slot_count
    return pl.pallas_call(
        functools.partial(embed_kernel, slot_count),
        in_specs=[pl.BlockSpec(memory_space=pltpu.HBM)] * 4,
        out_shape=(
            jax.ShapeDtypeStruct((width_all, width), BF16),
            jax.ShapeDtypeStruct((1, rows), jnp.int32),
        ),
        scratch_shapes=[
            pltpu.VMEM((rows, depth), BF16),
            pltpu.VMEM((depth, width), BF16),
            pltpu.VMEM((rows, width), F32),
            pltpu.VMEM((width_all, rows), BF16),
            pltpu.VMEM((1, rows), jnp.int32),
            pltpu.VMEM((rows,), jnp.int32),
            pltpu.SemaphoreType.DMA((steps,)),
            pltpu.SemaphoreType.DMA((steps,)),
            pltpu.SemaphoreType.DMA((2,)),
        ],
        compiler_params=pltpu.CompilerParams(vmem_limit_bytes=EMBED_VMEM_BYTES),
        cost_estimate=pl.CostEstimate(
            flops=2 * rows * depth * width, bytes_accessed=2 * depth * width + 2 * rows * depth, transcendentals=0
        ),
    )(tokens, weight, label_row, valid)


def score_kernel(slot_count, half, members_ref, message_ref, similar_hbm, gram, sem):
    width_all = members_ref.shape[0]
    owners, lanes = message_ref.shape
    block = width_all // 2
    copies = []
    nears, sums = [], []
    for b in range(2):
        part = slice(b * block, (b + 1) * block)
        gram[part, :] = lax.dot_general(
            members_ref[part, :], members_ref[...], (((1,), (1,)), ((), ())), preferred_element_type=F32
        )
        copy = pltpu.make_async_copy(gram.at[part, :], similar_hbm.at[0, part, :], sem.at[b])
        copy.start()
        copies.append(copy)
        tile = gram[part, :]
        own = lax.broadcasted_iota(jnp.int32, (block, width_all), 0) + b * block
        other = lax.broadcasted_iota(jnp.int32, (block, width_all), 1)
        nears.append(jnp.max(jnp.where(own == other, 0.0, tile), axis=1, keepdims=True))
        sums.append(jnp.sum(tile, axis=1, keepdims=True))
    near = jnp.concatenate(nears, axis=0)
    sums = jnp.concatenate(sums, axis=0)
    square = jnp.maximum(jnp.sum(sums, axis=0, keepdims=True), 0.0)
    dist = 1.0 - sums * lax.rsqrt(square + 1e-06)
    slot = lax.broadcasted_iota(jnp.int32, (width_all, lanes), 0)
    within = slot - (slot // slot_count) * slot_count
    lane = lax.broadcasted_iota(jnp.int32, (width_all, lanes), 1)
    spread = jnp.where(lane == within, near, jnp.where(lane == within + half, dist, 0.0))
    source = lax.broadcasted_iota(jnp.int32, (owners, width_all), 0) * slot_count
    member = lax.broadcasted_iota(jnp.int32, (owners, width_all), 1)
    chosen = jnp.where((member >= source) & (member < source + slot_count), 1.0, 0.0).astype(BF16)
    out = jnp.zeros((owners, lanes), F32)
    for piece in split3(spread):
        out += jnp.dot(chosen, piece, preferred_element_type=F32)
    message_ref[...] = out
    for copy in copies:
        copy.wait()


def scores(members, owners, slot_count, half):
    width_all, width = members.shape
    return pl.pallas_call(
        functools.partial(score_kernel, slot_count, half),
        out_specs=(pl.BlockSpec(memory_space=pltpu.VMEM), pl.BlockSpec(memory_space=pltpu.HBM)),
        out_shape=(
            jax.ShapeDtypeStruct((owners, 2 * half), F32),
            jax.ShapeDtypeStruct((1, width_all, width_all), F32),
        ),
        scratch_shapes=[pltpu.VMEM((width_all, width_all), F32), pltpu.SemaphoreType.DMA((2,))],
        compiler_params=pltpu.CompilerParams(vmem_limit_bytes=VMEM_BYTES),
    )(members)


def fetch_kernel(half, message_ref, label_ref, rank_ref, valid_ref, near_ref, dist_ref):
    owners, lanes = message_ref.shape
    rows = label_ref.shape[1]
    owner = lax.broadcasted_iota(jnp.int32, (owners, rows), 0)
    chosen = jnp.where(owner == label_ref[...], 1.0, 0.0).astype(BF16)
    mine = jnp.zeros((lanes, rows), F32)
    for piece in split3(message_ref[...]):
        mine += lax.dot_general(piece, chosen, (((0,), (0,)), ((), ())), preferred_element_type=F32)
    lane = lax.broadcasted_iota(jnp.int32, (lanes, rows), 0)
    rank = rank_ref[...]
    valid = valid_ref[...].astype(F32)
    near_ref[...] = jnp.sum(jnp.where(lane == rank, mine, 0.0), axis=0) * valid
    dist_ref[...] = jnp.sum(jnp.where(lane == rank + half, mine, 0.0), axis=0) * valid


def fetch(message, label_row, rank_row, valid, half):
    rows = label_row.shape[1]
    return pl.pallas_call(
        functools.partial(fetch_kernel, half),
        out_shape=(jax.ShapeDtypeStruct((rows,), F32),) * 2,
    )(message, label_row, rank_row, valid)


def per_device(tokens, proj_weight, labels, valid_rows):
    row_count = tokens.shape[0]
    owners = lax.axis_size("clus")
    slot_count = 2 * row_count // owners
    width_all = owners * slot_count
    half = -(-slot_count // 64) * 64
    label_row = labels.reshape(1, row_count)
    packed, rank_row = embed_and_pack(tokens, proj_weight, label_row, valid_rows, owners, slot_count)
    arrived = lax.all_to_all(
        packed.reshape(owners, slot_count, -1), "clus", split_axis=0, concat_axis=0, tiled=True
    )
    members = arrived.reshape(width_all, -1)
    message, similar = scores(members, owners, slot_count, half)
    returned = lax.all_to_all(message, "clus", split_axis=0, concat_axis=0, tiled=True)
    nearest, centre_dist = fetch(returned, label_row, rank_row, valid_rows, half)
    return (similar, nearest, centre_dist)


def solution(mesh):
    return jax.shard_map(
        per_device,
        mesh=mesh,
        in_specs=(
            P(("groups", "clus"), None),
            P(),
            P(("groups", "clus"), None),
            P(("groups", "clus")),
        ),
        out_specs=(P(("groups", "clus"), None, None), P(("groups", "clus")), P(("groups", "clus"))),
        check_vma=False,
    )
```

```python
import functools

import jax
import jax.numpy as jnp
from jax import lax
from jax.experimental import pallas as pl
from jax.experimental.pallas import tpu as pltpu
from jax.sharding import PartitionSpec as P

F32 = jnp.float32
BF16 = jnp.bfloat16
VMEM_BYTES = 48 * 1024 * 1024
EMBED_VMEM_BYTES = 55 * 1024 * 1024
LATE_VMEM_BYTES = 55 * 1024 * 1024
EARLY = 3
ORDER_FLOPS = 2 * 10**9


def split3(x):
    hi = x.astype(BF16)
    rest = x - hi.astype(F32)
    mid = rest.astype(BF16)
    low = (rest - mid.astype(F32)).astype(BF16)
    return hi, mid, low


def rank_rows(label_row):
    rows = label_row.shape[1]
    label = label_row.astype(F32)
    below = lax.broadcasted_iota(jnp.int32, (rows, rows), 0)
    across = lax.broadcasted_iota(jnp.int32, (rows, rows), 1)
    label_col = jnp.sum(jnp.where(below == across, label, 0.0), axis=1, keepdims=True)
    earlier = (label_col == label) & (below < across)
    return jnp.sum(jnp.where(earlier, 1.0, 0.0), axis=0, keepdims=True).astype(jnp.int32)


def place_rows(slot_row, valid_row, width_all):
    slots = lax.broadcasted_iota(jnp.int32, (width_all, slot_row.shape[1]), 0)
    slot = jnp.where(valid_row > 0, slot_row, -1)
    return jnp.where(slots == slot, 1.0, 0.0).astype(BF16)


def early_kernel(
    slot_count, tokens_hbm, weight_hbm, label_hbm, valid_hbm, keep_ref, send_ref, rank_ref, tokens,
    weight, total, place, label_ref, valid_ref, token_sem, weight_sem, small_sem,
):
    steps = token_sem.shape[0]
    block = tokens.shape[1] // steps
    early = weight.shape[1]
    small = (
        pltpu.make_async_copy(label_hbm, label_ref, small_sem.at[0]),
        pltpu.make_async_copy(valid_hbm, valid_ref, small_sem.at[1]),
    )
    for copy in small:
        copy.start()
    copies = []
    for k in range(steps):
        part = slice(k * block, (k + 1) * block)
        pair = (
            pltpu.make_async_copy(tokens_hbm.at[:, part], tokens.at[:, part], token_sem.at[k]),
            pltpu.make_async_copy(weight_hbm.at[part, 0:early], weight.at[part, :], weight_sem.at[k]),
        )
        for copy in pair:
            copy.start()
        copies.append(pair)
    for copy in small:
        copy.wait()
    rank = rank_rows(label_ref[...])
    rank_ref[...] = rank
    relative = (label_ref[...] ^ lax.axis_index("clus")) * slot_count + rank
    place[...] = place_rows(relative, valid_ref[...].reshape(label_ref.shape), place.shape[0])
    for k, pair in enumerate(copies):
        for copy in pair:
            copy.wait()
        part = slice(k * block, (k + 1) * block)
        product = jnp.dot(tokens[:, part], weight[part, :], preferred_element_type=F32)
        if k == 0:
            total[...] = product
        else:
            total[...] += product
    embed = total[...].astype(BF16)
    near = keep_ref.shape[0]
    send_ref[...] = jnp.dot(place[near:, :], embed, preferred_element_type=F32).astype(BF16)
    keep_ref[...] = jnp.dot(place[:near, :], embed, preferred_element_type=F32).astype(BF16)


def embed_early(tokens, weight, label_row, valid, owners, slot_count, early):
    rows, depth = tokens.shape
    steps = 4 if depth % 1024 == 0 else 1
    width_all = owners * slot_count
    return pl.pallas_call(
        functools.partial(early_kernel, slot_count),
        in_specs=[pl.BlockSpec(memory_space=pltpu.HBM)] * 4,
        out_specs=(pl.BlockSpec(memory_space=pltpu.VMEM),) * 4,
        out_shape=(
            jax.ShapeDtypeStruct((width_all // 2, early), BF16),
            jax.ShapeDtypeStruct((width_all // 2, early), BF16),
            jax.ShapeDtypeStruct((1, rows), jnp.int32),
            jax.ShapeDtypeStruct((rows, depth), BF16),
        ),
        scratch_shapes=[
            pltpu.VMEM((depth, early), BF16),
            pltpu.VMEM((rows, early), F32),
            pltpu.VMEM((width_all, rows), BF16),
            pltpu.VMEM((1, rows), jnp.int32),
            pltpu.VMEM((rows,), jnp.int32),
            pltpu.SemaphoreType.DMA((steps,)),
            pltpu.SemaphoreType.DMA((steps,)),
            pltpu.SemaphoreType.DMA((2,)),
        ],
        compiler_params=pltpu.CompilerParams(vmem_limit_bytes=EMBED_VMEM_BYTES),
        cost_estimate=pl.CostEstimate(
            flops=2 * rows * depth * early, bytes_accessed=2 * depth * early + 2 * rows * depth, transcendentals=0
        ),
    )(tokens, weight, label_row, valid)


def late_kernel(
    slot_count, tokens, weight_hbm, label_hbm, valid_hbm, rank_ref, packed_ref,
    weight, total, place, label_ref, valid_ref, weight_sem, small_sem,
):
    steps = weight_sem.shape[0]
    block = tokens.shape[1] // steps
    late = weight.shape[1]
    early = weight_hbm.shape[1] - late
    small = (
        pltpu.make_async_copy(label_hbm, label_ref, small_sem.at[0]),
        pltpu.make_async_copy(valid_hbm, valid_ref, small_sem.at[1]),
    )
    for copy in small:
        copy.start()
    copies = []
    for k in range(steps):
        part = slice(k * block, (k + 1) * block)
        copy = pltpu.make_async_copy(weight_hbm.at[part, early:early + late], weight.at[part, :], weight_sem.at[k])
        copy.start()
        copies.append(copy)
    for copy in small:
        copy.wait()
    slot = label_ref[...] * slot_count + rank_ref[...]
    place[...] = place_rows(slot, valid_ref[...].reshape(label_ref.shape), place.shape[0])
    for k, copy in enumerate(copies):
        copy.wait()
        part = slice(k * block, (k + 1) * block)
        product = jnp.dot(tokens[:, part], weight[part, :], preferred_element_type=F32)
        if k == 0:
            total[...] = product
        else:
            total[...] += product
    packed_ref[...] = jnp.dot(place[...], total[...].astype(BF16), preferred_element_type=F32).astype(BF16)


def embed_late(tokens, weight, label_row, valid, rank_row, owners, slot_count, early):
    rows, depth = tokens.shape
    late = weight.shape[1] - early
    steps = 8 if depth % 1024 == 0 else 1
    width_all = owners * slot_count
    return pl.pallas_call(
        functools.partial(late_kernel, slot_count),
        in_specs=[pl.BlockSpec(memory_space=pltpu.VMEM)]
        + [pl.BlockSpec(memory_space=pltpu.HBM)] * 3
        + [pl.BlockSpec(memory_space=pltpu.VMEM)],
        out_shape=jax.ShapeDtypeStruct((width_all, late), BF16),
        scratch_shapes=[
            pltpu.VMEM((depth, late), BF16),
            pltpu.VMEM((rows, late), F32),
            pltpu.VMEM((width_all, rows), BF16),
            pltpu.VMEM((1, rows), jnp.int32),
            pltpu.VMEM((rows,), jnp.int32),
            pltpu.SemaphoreType.DMA((steps,)),
            pltpu.SemaphoreType.DMA((2,)),
        ],
        compiler_params=pltpu.CompilerParams(vmem_limit_bytes=LATE_VMEM_BYTES),
        cost_estimate=pl.CostEstimate(
            flops=2 * rows * depth * late, bytes_accessed=2 * depth * late, transcendentals=0
        ),
    )(tokens, weight, label_row, valid, rank_row)


def spread_early(keep, send, owners, slot_count):
    early = keep.shape[1]
    held = keep.reshape(1, owners // 2, slot_count, early)
    leaving = send.reshape(1, owners // 2, slot_count, early)
    bit = owners // 2
    while bit:
        arrived = lax.ppermute(leaving, "clus", [(i, i ^ bit) for i in range(owners)])
        both = jnp.concatenate([held, arrived], axis=0)
        bit //= 2
        held, leaving = both[:, :bit], both[:, bit:]
    return both.reshape(owners * slot_count, early)


def order_kernel(slot_count, relative_ref, members_ref):
    width_all = relative_ref.shape[0]
    owners = width_all // slot_count
    me = lax.axis_index("clus")
    member = lax.broadcasted_iota(jnp.int32, (width_all, 1), 0)
    source = member // slot_count
    distance = source ^ me
    index = jnp.zeros_like(distance)
    low, high = 1, owners // 2
    while high:
        index += jnp.where((distance & low) > 0, high, 0)
        low, high = low * 2, high // 2
    wanted = index * slot_count + member - source * slot_count
    held = lax.broadcasted_iota(jnp.int32, (width_all, width_all), 1)
    chosen = jnp.where(held == wanted, 1.0, 0.0).astype(BF16)
    members_ref[...] = jnp.dot(chosen, relative_ref[...], preferred_element_type=F32).astype(BF16)


def order_early(relative, slot_count):
    return pl.pallas_call(
        functools.partial(order_kernel, slot_count),
        out_shape=jax.ShapeDtypeStruct(relative.shape, BF16),
        compiler_params=pltpu.CompilerParams(vmem_limit_bytes=VMEM_BYTES),
        cost_estimate=pl.CostEstimate(flops=ORDER_FLOPS, bytes_accessed=4 * relative.size, transcendentals=0),
    )(relative)


def score_kernel(slot_count, half, early_ref, late_ref, message_ref, similar_hbm, gram, sem):
    width_all = early_ref.shape[0]
    owners, lanes = message_ref.shape
    block = width_all // 2
    transposed = (((1,), (1,)), ((), ()))
    cols, rows = [], []
    for b in range(2):
        part = slice(b * block, (b + 1) * block)
        tile = lax.dot_general(early_ref[part, :], early_ref[...], transposed, preferred_element_type=F32)
        tile += lax.dot_general(late_ref[part, :], late_ref[...], transposed, preferred_element_type=F32)
        gram[part, :] = tile
        own = lax.broadcasted_iota(jnp.int32, (block, width_all), 0) + b * block
        other = lax.broadcasted_iota(jnp.int32, (block, width_all), 1)
        itself = jnp.where(own == other, tile, 0.0)
        cols.append(jnp.sum(itself, axis=1, keepdims=True))
        rows.append(jnp.sum(itself, axis=0, keepdims=True))
    scale_row = lax.rsqrt(rows[0] + rows[1] + 1e-06)
    copies = []
    nears, sums = [], []
    for b in range(2):
        part = slice(b * block, (b + 1) * block)
        scale_col = lax.rsqrt(cols[b] + 1e-06)
        tile = gram[part, :] * scale_col * scale_row
        gram[part, :] = tile
        copy = pltpu.make_async_copy(gram.at[part, :], similar_hbm.at[0, part, :], sem.at[b])
        copy.start()
        copies.append(copy)
        own = lax.broadcasted_iota(jnp.int32, (block, width_all), 0) + b * block
        other = lax.broadcasted_iota(jnp.int32, (block, width_all), 1)
        nears.append(jnp.max(jnp.where(own == other, 0.0, tile), axis=1, keepdims=True))
        sums.append(jnp.sum(tile, axis=1, keepdims=True))
    near = jnp.concatenate(nears, axis=0)
    sums = jnp.concatenate(sums, axis=0)
    square = jnp.maximum(jnp.sum(sums, axis=0, keepdims=True), 0.0)
    dist = 1.0 - sums * lax.rsqrt(square + 1e-06)
    slot = lax.broadcasted_iota(jnp.int32, (width_all, lanes), 0)
    within = slot - (slot // slot_count) * slot_count
    lane = lax.broadcasted_iota(jnp.int32, (width_all, lanes), 1)
    spread = jnp.where(lane == within, near, jnp.where(lane == within + half, dist, 0.0))
    source = lax.broadcasted_iota(jnp.int32, (owners, width_all), 0) * slot_count
    member = lax.broadcasted_iota(jnp.int32, (owners, width_all), 1)
    chosen = jnp.where((member >= source) & (member < source + slot_count), 1.0, 0.0).astype(BF16)
    out = jnp.zeros((owners, lanes), F32)
    for piece in split3(spread):
        out += jnp.dot(chosen, piece, preferred_element_type=F32)
    message_ref[...] = out
    for copy in copies:
        copy.wait()


def scores(early, late, owners, slot_count, half):
    width_all = early.shape[0]
    return pl.pallas_call(
        functools.partial(score_kernel, slot_count, half),
        out_specs=(pl.BlockSpec(memory_space=pltpu.VMEM), pl.BlockSpec(memory_space=pltpu.HBM)),
        out_shape=(
            jax.ShapeDtypeStruct((owners, 2 * half), F32),
            jax.ShapeDtypeStruct((1, width_all, width_all), F32),
        ),
        scratch_shapes=[pltpu.VMEM((width_all, width_all), F32), pltpu.SemaphoreType.DMA((2,))],
        compiler_params=pltpu.CompilerParams(vmem_limit_bytes=VMEM_BYTES),
    )(early, late)


def fetch_kernel(half, message_ref, label_ref, rank_ref, valid_ref, near_ref, dist_ref):
    owners, lanes = message_ref.shape
    rows = label_ref.shape[1]
    owner = lax.broadcasted_iota(jnp.int32, (owners, rows), 0)
    chosen = jnp.where(owner == label_ref[...], 1.0, 0.0).astype(BF16)
    mine = jnp.zeros((lanes, rows), F32)
    for piece in split3(message_ref[...]):
        mine += lax.dot_general(piece, chosen, (((0,), (0,)), ((), ())), preferred_element_type=F32)
    lane = lax.broadcasted_iota(jnp.int32, (lanes, rows), 0)
    rank = rank_ref[...]
    valid = valid_ref[...].astype(F32)
    near_ref[...] = jnp.sum(jnp.where(lane == rank, mine, 0.0), axis=0) * valid
    dist_ref[...] = jnp.sum(jnp.where(lane == rank + half, mine, 0.0), axis=0) * valid


def fetch(message, label_row, rank_row, valid, half):
    rows = label_row.shape[1]
    return pl.pallas_call(
        functools.partial(fetch_kernel, half),
        out_shape=(jax.ShapeDtypeStruct((rows,), F32),) * 2,
    )(message, label_row, rank_row, valid)


def per_device(tokens, proj_weight, labels, valid_rows):
    row_count = tokens.shape[0]
    owners = lax.axis_size("clus")
    slot_count = 2 * row_count // owners
    width_all = owners * slot_count
    half = -(-slot_count // 64) * 64
    early = EARLY * proj_weight.shape[1] // 8
    label_row = labels.reshape(1, row_count)
    keep, send, rank_row, held_tokens = embed_early(
        tokens, proj_weight, label_row, valid_rows, owners, slot_count, early
    )
    packed = embed_late(held_tokens, proj_weight, label_row, valid_rows, rank_row, owners, slot_count, early)
    arrived = lax.all_to_all(
        packed.reshape(owners, slot_count, -1), "clus", split_axis=0, concat_axis=0, tiled=True
    )
    early_members = order_early(spread_early(keep, send, owners, slot_count), slot_count)
    message, similar = scores(early_members, arrived.reshape(width_all, -1), owners, slot_count, half)
    returned = lax.all_to_all(message, "clus", split_axis=0, concat_axis=0, tiled=True)
    nearest, centre_dist = fetch(returned, label_row, rank_row, valid_rows, half)
    return (similar, nearest, centre_dist)


def solution(mesh):
    return jax.shard_map(
        per_device,
        mesh=mesh,
        in_specs=(
            P(("groups", "clus"), None),
            P(),
            P(("groups", "clus"), None),
            P(("groups", "clus")),
        ),
        out_specs=(P(("groups", "clus"), None, None), P(("groups", "clus")), P(("groups", "clus"))),
        check_vma=False,
    )
```

```python
import functools

import jax
import jax.numpy as jnp
from jax import lax
from jax.experimental import pallas as pl
from jax.experimental.pallas import tpu as pltpu
from jax.sharding import PartitionSpec as P

F32 = jnp.float32
BF16 = jnp.bfloat16
VMEM_BYTES = 48 * 1024 * 1024
EMBED_VMEM_BYTES = 60 * 1024 * 1024
EARLY = 1
ORDER_FLOPS = 15000000000


def split3(x):
    hi = x.astype(BF16)
    rest = x - hi.astype(F32)
    mid = rest.astype(BF16)
    low = (rest - mid.astype(F32)).astype(BF16)
    return hi, mid, low


def rank_rows(label_row):
    rows = label_row.shape[1]
    label = label_row.astype(F32)
    below = lax.broadcasted_iota(jnp.int32, (rows, rows), 0)
    across = lax.broadcasted_iota(jnp.int32, (rows, rows), 1)
    label_col = jnp.sum(jnp.where(below == across, label, 0.0), axis=1, keepdims=True)
    earlier = (label_col == label) & (below < across)
    return jnp.sum(jnp.where(earlier, 1.0, 0.0), axis=0, keepdims=True).astype(jnp.int32)


def place_rows(slot_row, valid_row, width_all):
    slots = lax.broadcasted_iota(jnp.int32, (width_all, slot_row.shape[1]), 0)
    slot = jnp.where(valid_row > 0, slot_row, -1)
    return jnp.where(slots == slot, 1.0, 0.0).astype(BF16)


def exchange_bits(owners):
    bits = []
    bit = owners // 2
    while bit:
        bits.append(bit)
        bit //= 2
    return bits[:1] + bits[2:] + bits[1:2]


def embed_kernel(
    slot_count, bits, tokens_hbm, weight_hbm, label_hbm, valid_hbm, keep_ref, send_ref, packed_ref, rank_ref,
    tokens, weight, total, place, apart, label_ref, valid_ref, token_sem, weight_sem, small_sem,
):
    steps = token_sem.shape[0]
    block = tokens.shape[1] // steps
    early = keep_ref.shape[1]
    small = (
        pltpu.make_async_copy(label_hbm, label_ref, small_sem.at[0]),
        pltpu.make_async_copy(valid_hbm, valid_ref, small_sem.at[1]),
    )
    for copy in small:
        copy.start()
    copies = []
    for k in range(steps):
        part = slice(k * block, (k + 1) * block)
        copies.append((
            pltpu.make_async_copy(tokens_hbm.at[:, part], tokens.at[:, part], token_sem.at[k]),
            pltpu.make_async_copy(weight_hbm.at[part, :], weight.at[part, :], weight_sem.at[k]),
        ))
    for pair in copies[:2]:
        for copy in pair:
            copy.start()
    for copy in small:
        copy.wait()
    label = label_ref[...]
    valid = valid_ref[...].reshape(label.shape)
    rank = rank_rows(label)
    rank_ref[...] = rank
    place[...] = place_rows(label * slot_count + rank, valid, place.shape[0])
    distance = label ^ lax.axis_index("clus")
    position = jnp.zeros_like(label)
    for k, bit in enumerate(bits):
        position += jnp.where((distance & bit) > 0, 1 << (len(bits) - 1 - k), 0)
    apart[...] = place_rows(position * slot_count + rank, valid, place.shape[0])
    for k, pair in enumerate(copies):
        for copy in pair:
            copy.wait()
        for copy in (copies[k + 2] if k + 2 < steps else ()):
            copy.start()
        part = slice(k * block, (k + 1) * block)
        product = jnp.dot(tokens[:, part], weight[part, :], preferred_element_type=F32)
        if k == 0:
            total[...] = product
        else:
            total[...] += product
    embed = total[...]
    scale = lax.rsqrt(jnp.sum(embed * embed, axis=1, keepdims=True) + 1e-06)
    near = keep_ref.shape[0]
    unit = (total[:, :early] * scale).astype(BF16)
    send_ref[...] = jnp.dot(apart[near:, :], unit, preferred_element_type=F32).astype(BF16)
    keep_ref[...] = jnp.dot(apart[:near, :], unit, preferred_element_type=F32).astype(BF16)
    unit = (total[:, early:] * scale).astype(BF16)
    packed_ref[...] = jnp.dot(place[...], unit, preferred_element_type=F32).astype(BF16)


def embed_and_pack(tokens, weight, label_row, valid, owners, slot_count, early):
    rows, depth = tokens.shape
    width = weight.shape[1]
    steps = 4 if depth % 512 == 0 else 1
    width_all = owners * slot_count
    return pl.pallas_call(
        functools.partial(embed_kernel, slot_count, exchange_bits(owners)),
        in_specs=[pl.BlockSpec(memory_space=pltpu.HBM)] * 4,
        out_shape=(
            jax.ShapeDtypeStruct((width_all // 2, early), BF16),
            jax.ShapeDtypeStruct((width_all // 2, early), BF16),
            jax.ShapeDtypeStruct((width_all, width - early), BF16),
            jax.ShapeDtypeStruct((1, rows), jnp.int32),
        ),
        scratch_shapes=[
            pltpu.VMEM((rows, depth), BF16),
            pltpu.VMEM((depth, width), BF16),
            pltpu.VMEM((rows, width), F32),
            pltpu.VMEM((width_all, rows), BF16),
            pltpu.VMEM((width_all, rows), BF16),
            pltpu.VMEM((1, rows), jnp.int32),
            pltpu.VMEM((rows,), jnp.int32),
            pltpu.SemaphoreType.DMA((steps,)),
            pltpu.SemaphoreType.DMA((steps,)),
            pltpu.SemaphoreType.DMA((2,)),
        ],
        compiler_params=pltpu.CompilerParams(vmem_limit_bytes=EMBED_VMEM_BYTES),
        cost_estimate=pl.CostEstimate(
            flops=2 * rows * depth * width, bytes_accessed=2 * depth * width + 2 * rows * depth, transcendentals=0
        ),
    )(tokens, weight, label_row, valid)


def spread_early(keep, send, owners, slot_count):
    early = keep.shape[1]
    left = owners // 2
    held = keep.reshape(1, left, slot_count, early)
    leaving = send.reshape(1, left, slot_count, early)
    for bit in exchange_bits(owners):
        arrived = lax.ppermute(leaving, "clus", [(i, i ^ bit) for i in range(owners)])
        both = jnp.concatenate([held, arrived], axis=0)
        left //= 2
        held, leaving = both[:, :left], both[:, left:]
    return both.reshape(owners * slot_count, early)


def order_kernel(slot_count, bits, relative_ref, members_ref):
    width_all = relative_ref.shape[0]
    member = lax.broadcasted_iota(jnp.int32, (width_all, 1), 0)
    source = member // slot_count
    distance = source ^ lax.axis_index("clus")
    index = jnp.zeros_like(distance)
    for k, bit in enumerate(bits):
        index += jnp.where((distance & bit) > 0, 1 << k, 0)
    wanted = index * slot_count + member - source * slot_count
    held = lax.broadcasted_iota(jnp.int32, (width_all, width_all), 1)
    chosen = jnp.where(held == wanted, 1.0, 0.0).astype(BF16)
    members_ref[...] = jnp.dot(chosen, relative_ref[...], preferred_element_type=F32).astype(BF16)


def order_early(relative, owners, slot_count):
    return pl.pallas_call(
        functools.partial(order_kernel, slot_count, exchange_bits(owners)),
        out_shape=jax.ShapeDtypeStruct(relative.shape, BF16),
        compiler_params=pltpu.CompilerParams(vmem_limit_bytes=VMEM_BYTES),
        cost_estimate=pl.CostEstimate(flops=ORDER_FLOPS, bytes_accessed=4 * relative.size, transcendentals=0),
    )(relative)


def score_kernel(slot_count, half, early_ref, late_ref, message_ref, similar_hbm, gram, sem):
    width_all = early_ref.shape[0]
    transposed = (((1,), (1,)), ((), ()))
    owners, lanes = message_ref.shape
    block = width_all // 2
    copies = []
    nears, sums = [], []
    for b in range(2):
        part = slice(b * block, (b + 1) * block)
        tile = lax.dot_general(early_ref[part, :], early_ref[...], transposed, preferred_element_type=F32)
        tile += lax.dot_general(late_ref[part, :], late_ref[...], transposed, preferred_element_type=F32)
        gram[part, :] = tile
        copy = pltpu.make_async_copy(gram.at[part, :], similar_hbm.at[0, part, :], sem.at[b])
        copy.start()
        copies.append(copy)
        own = lax.broadcasted_iota(jnp.int32, (block, width_all), 0) + b * block
        other = lax.broadcasted_iota(jnp.int32, (block, width_all), 1)
        nears.append(jnp.max(jnp.where(own == other, 0.0, tile), axis=1, keepdims=True))
        sums.append(jnp.sum(tile, axis=1, keepdims=True))
    near = jnp.concatenate(nears, axis=0)
    sums = jnp.concatenate(sums, axis=0)
    square = jnp.maximum(jnp.sum(sums, axis=0, keepdims=True), 0.0)
    dist = 1.0 - sums * lax.rsqrt(square + 1e-06)
    slot = lax.broadcasted_iota(jnp.int32, (width_all, lanes), 0)
    within = slot - (slot // slot_count) * slot_count
    lane = lax.broadcasted_iota(jnp.int32, (width_all, lanes), 1)
    spread = jnp.where(lane == within, near, jnp.where(lane == within + half, dist, 0.0))
    source = lax.broadcasted_iota(jnp.int32, (owners, width_all), 0) * slot_count
    member = lax.broadcasted_iota(jnp.int32, (owners, width_all), 1)
    chosen = jnp.where((member >= source) & (member < source + slot_count), 1.0, 0.0).astype(BF16)
    out = jnp.zeros((owners, lanes), F32)
    for piece in split3(spread):
        out += jnp.dot(chosen, piece, preferred_element_type=F32)
    message_ref[...] = out
    for copy in copies:
        copy.wait()


def scores(early, late, owners, slot_count, half):
    width_all = early.shape[0]
    return pl.pallas_call(
        functools.partial(score_kernel, slot_count, half),
        out_specs=(pl.BlockSpec(memory_space=pltpu.VMEM), pl.BlockSpec(memory_space=pltpu.HBM)),
        out_shape=(
            jax.ShapeDtypeStruct((owners, 2 * half), F32),
            jax.ShapeDtypeStruct((1, width_all, width_all), F32),
        ),
        scratch_shapes=[pltpu.VMEM((width_all, width_all), F32), pltpu.SemaphoreType.DMA((2,))],
        compiler_params=pltpu.CompilerParams(vmem_limit_bytes=VMEM_BYTES),
    )(early, late)


def fetch_kernel(half, message_ref, label_ref, rank_ref, valid_ref, near_ref, dist_ref):
    owners, lanes = message_ref.shape
    rows = label_ref.shape[1]
    owner = lax.broadcasted_iota(jnp.int32, (owners, rows), 0)
    chosen = jnp.where(owner == label_ref[...], 1.0, 0.0).astype(BF16)
    mine = jnp.zeros((lanes, rows), F32)
    for piece in split3(message_ref[...]):
        mine += lax.dot_general(piece, chosen, (((0,), (0,)), ((), ())), preferred_element_type=F32)
    lane = lax.broadcasted_iota(jnp.int32, (lanes, rows), 0)
    rank = rank_ref[...]
    valid = valid_ref[...].astype(F32)
    near_ref[...] = jnp.sum(jnp.where(lane == rank, mine, 0.0), axis=0) * valid
    dist_ref[...] = jnp.sum(jnp.where(lane == rank + half, mine, 0.0), axis=0) * valid


def fetch(message, label_row, rank_row, valid, half):
    rows = label_row.shape[1]
    return pl.pallas_call(
        functools.partial(fetch_kernel, half),
        out_shape=(jax.ShapeDtypeStruct((rows,), F32),) * 2,
    )(message, label_row, rank_row, valid)


def per_device(tokens, proj_weight, labels, valid_rows):
    row_count = tokens.shape[0]
    owners = lax.axis_size("clus")
    slot_count = 2 * row_count // owners
    width_all = owners * slot_count
    half = -(-slot_count // 64) * 64
    early = EARLY * proj_weight.shape[1] // 8
    label_row = labels.reshape(1, row_count)
    keep, send, packed, rank_row = embed_and_pack(
        tokens, proj_weight, label_row, valid_rows, owners, slot_count, early
    )
    arrived = lax.all_to_all(
        packed.reshape(owners, slot_count, -1), "clus", split_axis=0, concat_axis=0, tiled=True
    )
    early_members = order_early(spread_early(keep, send, owners, slot_count), owners, slot_count)
    message, similar = scores(early_members, arrived.reshape(width_all, -1), owners, slot_count, half)
    returned = lax.all_to_all(message, "clus", split_axis=0, concat_axis=0, tiled=True)
    nearest, centre_dist = fetch(returned, label_row, rank_row, valid_rows, half)
    return (similar, nearest, centre_dist)


def solution(mesh):
    return jax.shard_map(
        per_device,
        mesh=mesh,
        in_specs=(
            P(("groups", "clus"), None),
            P(),
            P(("groups", "clus"), None),
            P(("groups", "clus")),
        ),
        out_specs=(P(("groups", "clus"), None, None), P(("groups", "clus")), P(("groups", "clus"))),
        check_vma=False,
    )
```

```python
import functools

import jax
import jax.numpy as jnp
from jax import lax
from jax.experimental import pallas as pl
from jax.experimental.pallas import tpu as pltpu
from jax.sharding import PartitionSpec as P

F32 = jnp.float32
BF16 = jnp.bfloat16
VMEM_BYTES = 48 * 1024 * 1024
EMBED_VMEM_BYTES = 60 * 1024 * 1024
FETCH_VMEM_BYTES = 8 * 1024 * 1024
EARLY = 2
ORDER_FLOPS = 13 * 10**9


def split3(x):
    hi = x.astype(BF16)
    rest = x - hi.astype(F32)
    mid = rest.astype(BF16)
    low = (rest - mid.astype(F32)).astype(BF16)
    return hi, mid, low


def rank_rows(label_row):
    rows = label_row.shape[1]
    label = label_row.astype(F32)
    below = lax.broadcasted_iota(jnp.int32, (rows, rows), 0)
    across = lax.broadcasted_iota(jnp.int32, (rows, rows), 1)
    label_col = jnp.sum(jnp.where(below == across, label, 0.0), axis=1, keepdims=True)
    earlier = (label_col == label) & (below < across)
    return jnp.sum(jnp.where(earlier, 1.0, 0.0), axis=0, keepdims=True).astype(jnp.int32)


def place_rows(slot_row, valid_row, width_all):
    slots = lax.broadcasted_iota(jnp.int32, (width_all, slot_row.shape[1]), 0)
    slot = jnp.where(valid_row > 0, slot_row, -1)
    return jnp.where(slots == slot, 1.0, 0.0).astype(BF16)


def exchange_bits(owners):
    middle = []
    bit = 1
    while bit < owners // 8:
        middle.append(bit)
        bit *= 2
    return [owners // 2] + middle + [owners // 8, owners // 4]


def embed_kernel(
    slot_count, bits, tokens_hbm, weight_hbm, label_hbm, valid_hbm, keep_ref, send_ref, packed_ref, rank_ref,
    tokens, weight, total, place, apart, label_ref, valid_ref, token_sem, weight_sem, small_sem,
):
    steps = token_sem.shape[0]
    block = tokens.shape[1] // steps
    early = keep_ref.shape[1]
    small = (
        pltpu.make_async_copy(label_hbm, label_ref, small_sem.at[0]),
        pltpu.make_async_copy(valid_hbm, valid_ref, small_sem.at[1]),
    )
    for copy in small:
        copy.start()
    copies = []
    for k in range(steps):
        part = slice(k * block, (k + 1) * block)
        copies.append((
            pltpu.make_async_copy(tokens_hbm.at[:, part], tokens.at[:, part], token_sem.at[k]),
            pltpu.make_async_copy(weight_hbm.at[part, :], weight.at[part, :], weight_sem.at[k]),
        ))
    for pair in copies[:2]:
        for copy in pair:
            copy.start()
    for copy in small:
        copy.wait()
    label = label_ref[...]
    valid = valid_ref[...].reshape(label.shape)
    rank = rank_rows(label)
    rank_ref[...] = rank
    place[...] = place_rows(label * slot_count + rank, valid, place.shape[0])
    distance = label ^ lax.axis_index("clus")
    position = jnp.zeros_like(label)
    for k, bit in enumerate(bits):
        position += jnp.where((distance & bit) > 0, 1 << (len(bits) - 1 - k), 0)
    apart[...] = place_rows(position * slot_count + rank, valid, place.shape[0])
    for k, pair in enumerate(copies):
        for copy in pair:
            copy.wait()
        for copy in (copies[k + 2] if k + 2 < steps else ()):
            copy.start()
        part = slice(k * block, (k + 1) * block)
        product = jnp.dot(tokens[:, part], weight[part, :], preferred_element_type=F32)
        if k == 0:
            total[...] = product
        else:
            total[...] += product
    embed = total[...]
    scale = lax.rsqrt(jnp.sum(embed * embed, axis=1, keepdims=True) + 1e-06)
    near = keep_ref.shape[0]
    unit = (total[:, :early] * scale).astype(BF16)
    send_ref[...] = jnp.dot(apart[near:, :], unit, preferred_element_type=F32).astype(BF16)
    keep_ref[...] = jnp.dot(apart[:near, :], unit, preferred_element_type=F32).astype(BF16)
    unit = (total[:, early:] * scale).astype(BF16)
    packed_ref[...] = jnp.dot(place[...], unit, preferred_element_type=F32).astype(BF16)


def embed_and_pack(tokens, weight, label_row, valid, owners, slot_count, early):
    rows, depth = tokens.shape
    width = weight.shape[1]
    steps = 4 if depth % 512 == 0 else 1
    width_all = owners * slot_count
    return pl.pallas_call(
        functools.partial(embed_kernel, slot_count, exchange_bits(owners)),
        in_specs=[pl.BlockSpec(memory_space=pltpu.HBM)] * 4,
        out_shape=(
            jax.ShapeDtypeStruct((width_all // 2, early), BF16),
            jax.ShapeDtypeStruct((width_all // 2, early), BF16),
            jax.ShapeDtypeStruct((width_all, width - early), BF16),
            jax.ShapeDtypeStruct((1, rows), jnp.int32),
        ),
        scratch_shapes=[
            pltpu.VMEM((rows, depth), BF16),
            pltpu.VMEM((depth, width), BF16),
            pltpu.VMEM((rows, width), F32),
            pltpu.VMEM((width_all, rows), BF16),
            pltpu.VMEM((width_all, rows), BF16),
            pltpu.VMEM((1, rows), jnp.int32),
            pltpu.VMEM((rows,), jnp.int32),
            pltpu.SemaphoreType.DMA((steps,)),
            pltpu.SemaphoreType.DMA((steps,)),
            pltpu.SemaphoreType.DMA((2,)),
        ],
        compiler_params=pltpu.CompilerParams(vmem_limit_bytes=EMBED_VMEM_BYTES),
        cost_estimate=pl.CostEstimate(
            flops=2 * rows * depth * width, bytes_accessed=2 * depth * width + 2 * rows * depth, transcendentals=0
        ),
    )(tokens, weight, label_row, valid)


def spread_early(keep, send, owners, slot_count):
    early = keep.shape[1]
    *bits, low, high = exchange_bits(owners)
    left = owners // 2
    held = keep.reshape(1, left, slot_count, early)
    leaving = send.reshape(1, left, slot_count, early)
    for bit in bits:
        arrived = lax.ppermute(leaving, "clus", [(i, i ^ bit) for i in range(owners)])
        both = jnp.concatenate([held, arrived], axis=0)
        left //= 2
        held, leaving = both[:, :left], both[:, left:]
    blocks = [both[:, k] for k in range(4)]
    parts = [blocks[0]]
    for block, mask in ((blocks[2], low), (blocks[1], high), (blocks[3], low | high)):
        parts.append(lax.ppermute(block, "clus", [(i, i ^ mask) for i in range(owners)]))
    return jnp.concatenate(parts, axis=0).reshape(owners * slot_count, early)


def order_kernel(slot_count, bits, relative_ref, members_ref):
    width_all = relative_ref.shape[0]
    member = lax.broadcasted_iota(jnp.int32, (width_all, 1), 0)
    source = member // slot_count
    distance = source ^ lax.axis_index("clus")
    index = jnp.zeros_like(distance)
    for k, bit in enumerate(bits):
        index += jnp.where((distance & bit) > 0, 1 << k, 0)
    wanted = index * slot_count + member - source * slot_count
    held = lax.broadcasted_iota(jnp.int32, (width_all, width_all), 1)
    chosen = jnp.where(held == wanted, 1.0, 0.0).astype(BF16)
    members_ref[...] = jnp.dot(chosen, relative_ref[...], preferred_element_type=F32).astype(BF16)


def order_early(relative, owners, slot_count):
    return pl.pallas_call(
        functools.partial(order_kernel, slot_count, exchange_bits(owners)),
        out_shape=jax.ShapeDtypeStruct(relative.shape, BF16),
        compiler_params=pltpu.CompilerParams(vmem_limit_bytes=VMEM_BYTES),
        cost_estimate=pl.CostEstimate(flops=ORDER_FLOPS, bytes_accessed=4 * relative.size, transcendentals=0),
    )(relative)


def score_kernel(slot_count, half, early_ref, late_ref, message_ref, similar_hbm, gram, sem):
    width_all = early_ref.shape[0]
    transposed = (((1,), (1,)), ((), ()))
    owners, lanes = message_ref.shape
    block = width_all // 2
    copies = []
    nears, sums = [], []
    for b in range(2):
        part = slice(b * block, (b + 1) * block)
        tile = lax.dot_general(early_ref[part, :], early_ref[...], transposed, preferred_element_type=F32)
        tile += lax.dot_general(late_ref[part, :], late_ref[...], transposed, preferred_element_type=F32)
        gram[part, :] = tile
        copy = pltpu.make_async_copy(gram.at[part, :], similar_hbm.at[0, part, :], sem.at[b])
        copy.start()
        copies.append(copy)
        own = lax.broadcasted_iota(jnp.int32, (block, width_all), 0) + b * block
        other = lax.broadcasted_iota(jnp.int32, (block, width_all), 1)
        nears.append(jnp.max(jnp.where(own == other, 0.0, tile), axis=0, keepdims=True))
        sums.append(jnp.sum(tile, axis=0, keepdims=True))
    near = jnp.maximum(nears[0], nears[1])
    total = sums[0] + sums[1]
    square = jnp.maximum(jnp.sum(total, axis=1, keepdims=True), 0.0)
    dist = 1.0 - total * lax.rsqrt(square + 1e-06)
    slot = lax.broadcasted_iota(jnp.int32, (width_all, lanes), 0)
    within = slot - (slot // slot_count) * slot_count
    lane = lax.broadcasted_iota(jnp.int32, (width_all, lanes), 1)
    source = lax.broadcasted_iota(jnp.int32, (owners, width_all), 0) * slot_count
    member = lax.broadcasted_iota(jnp.int32, (owners, width_all), 1)
    mine = (member >= source) & (member < source + slot_count)
    out = jnp.zeros((owners, lanes), F32)
    for values, start in ((near, 0), (dist, half)):
        chosen = jnp.where(lane == within + start, 1.0, 0.0).astype(BF16)
        for piece in split3(jnp.where(mine, values, 0.0)):
            out += jnp.dot(piece, chosen, preferred_element_type=F32)
    message_ref[...] = out
    for copy in copies:
        copy.wait()


def scores(early, late, owners, slot_count, half):
    width_all = early.shape[0]
    return pl.pallas_call(
        functools.partial(score_kernel, slot_count, half),
        out_specs=(pl.BlockSpec(memory_space=pltpu.VMEM), pl.BlockSpec(memory_space=pltpu.HBM)),
        out_shape=(
            jax.ShapeDtypeStruct((owners, 2 * half), F32),
            jax.ShapeDtypeStruct((1, width_all, width_all), F32),
        ),
        scratch_shapes=[pltpu.VMEM((width_all, width_all), F32), pltpu.SemaphoreType.DMA((2,))],
        compiler_params=pltpu.CompilerParams(vmem_limit_bytes=VMEM_BYTES),
    )(early, late)


def fetch_kernel(half, message_ref, label_ref, rank_ref, valid_ref, near_ref, dist_ref):
    owners, lanes = message_ref.shape
    rows = label_ref.shape[1]
    owner = lax.broadcasted_iota(jnp.int32, (owners, rows), 0)
    chosen = jnp.where(owner == label_ref[...], 1.0, 0.0).astype(BF16)
    mine = jnp.zeros((lanes, rows), F32)
    for piece in split3(message_ref[...]):
        mine += lax.dot_general(piece, chosen, (((0,), (0,)), ((), ())), preferred_element_type=F32)
    lane = lax.broadcasted_iota(jnp.int32, (lanes, rows), 0)
    rank = rank_ref[...]
    valid = valid_ref[...].astype(F32)
    near_ref[...] = jnp.sum(jnp.where(lane == rank, mine, 0.0), axis=0) * valid
    dist_ref[...] = jnp.sum(jnp.where(lane == rank + half, mine, 0.0), axis=0) * valid


def fetch(message, label_row, rank_row, valid, half):
    rows = label_row.shape[1]
    return pl.pallas_call(
        functools.partial(fetch_kernel, half),
        out_shape=(jax.ShapeDtypeStruct((rows,), F32),) * 2,
        compiler_params=pltpu.CompilerParams(vmem_limit_bytes=FETCH_VMEM_BYTES),
    )(message, label_row, rank_row, valid)


def per_device(tokens, proj_weight, labels, valid_rows):
    row_count = tokens.shape[0]
    owners = lax.axis_size("clus")
    slot_count = 2 * row_count // owners
    width_all = owners * slot_count
    half = -(-slot_count // 64) * 64
    early = EARLY * proj_weight.shape[1] // 8
    label_row = labels.reshape(1, row_count)
    keep, send, packed, rank_row = embed_and_pack(
        tokens, proj_weight, label_row, valid_rows, owners, slot_count, early
    )
    arrived = lax.all_to_all(
        packed.reshape(owners, slot_count, -1), "clus", split_axis=0, concat_axis=0, tiled=True
    )
    early_members = order_early(spread_early(keep, send, owners, slot_count), owners, slot_count)
    message, similar = scores(early_members, arrived.reshape(width_all, -1), owners, slot_count, half)
    returned = lax.all_to_all(message, "clus", split_axis=0, concat_axis=0, tiled=True)
    nearest, centre_dist = fetch(returned, label_row, rank_row, valid_rows, half)
    return (similar, nearest, centre_dist)


def solution(mesh):
    return jax.shard_map(
        per_device,
        mesh=mesh,
        in_specs=(
            P(("groups", "clus"), None),
            P(),
            P(("groups", "clus"), None),
            P(("groups", "clus")),
        ),
        out_specs=(P(("groups", "clus"), None, None), P(("groups", "clus")), P(("groups", "clus"))),
        check_vma=False,
    )
```

```python
import functools

import jax
import jax.numpy as jnp
from jax import lax
from jax.experimental import pallas as pl
from jax.experimental.pallas import tpu as pltpu
from jax.sharding import PartitionSpec as P

F32 = jnp.float32
BF16 = jnp.bfloat16
VMEM_BYTES = 48 * 1024 * 1024
EMBED_VMEM_BYTES = 40 * 1024 * 1024
PACK_VMEM_BYTES = 16 * 1024 * 1024
FETCH_VMEM_BYTES = 8 * 1024 * 1024
EARLY = 2
ORDER_FLOPS = 13 * 10**9


def split3(x):
    hi = x.astype(BF16)
    rest = x - hi.astype(F32)
    mid = rest.astype(BF16)
    low = (rest - mid.astype(F32)).astype(BF16)
    return hi, mid, low


def rank_rows(label_row):
    rows = label_row.shape[1]
    label = label_row.astype(F32)
    below = lax.broadcasted_iota(jnp.int32, (rows, rows), 0)
    across = lax.broadcasted_iota(jnp.int32, (rows, rows), 1)
    label_col = jnp.sum(jnp.where(below == across, label, 0.0), axis=1, keepdims=True)
    earlier = (label_col == label) & (below < across)
    return jnp.sum(jnp.where(earlier, 1.0, 0.0), axis=0, keepdims=True).astype(jnp.int32)


def place_rows(slot_row, valid_row, width_all):
    slots = lax.broadcasted_iota(jnp.int32, (width_all, slot_row.shape[1]), 0)
    slot = jnp.where(valid_row > 0, slot_row, -1)
    return jnp.where(slots == slot, 1.0, 0.0).astype(BF16)


def exchange_bits(owners):
    middle = []
    bit = 1
    while bit < owners // 8:
        middle.append(bit)
        bit *= 2
    return [owners // 2] + middle + [owners // 8, owners // 4]


def embed_kernel(
    slot_count, bits, tokens_hbm, weight_hbm, label_hbm, valid_hbm, keep_ref, send_ref, place, late_ref, rank_ref,
    tokens, weight, total, apart, label_ref, valid_ref, token_sem, weight_sem, small_sem,
):
    steps = token_sem.shape[0]
    block = tokens.shape[1] // steps
    early = keep_ref.shape[1]
    small = (
        pltpu.make_async_copy(label_hbm, label_ref, small_sem.at[0]),
        pltpu.make_async_copy(valid_hbm, valid_ref, small_sem.at[1]),
    )
    for copy in small:
        copy.start()
    copies = []
    for k in range(steps):
        part = slice(k * block, (k + 1) * block)
        copies.append((
            pltpu.make_async_copy(tokens_hbm.at[:, part], tokens.at[:, part], token_sem.at[k]),
            pltpu.make_async_copy(weight_hbm.at[part, :], weight.at[part, :], weight_sem.at[k]),
        ))
    for pair in copies[:2]:
        for copy in pair:
            copy.start()
    for copy in small:
        copy.wait()
    label = label_ref[...]
    valid = valid_ref[...].reshape(label.shape)
    rank = rank_rows(label)
    rank_ref[...] = rank
    place[...] = place_rows(label * slot_count + rank, valid, place.shape[0])
    distance = label ^ lax.axis_index("clus")
    position = jnp.zeros_like(label)
    for k, bit in enumerate(bits):
        position += jnp.where((distance & bit) > 0, 1 << (len(bits) - 1 - k), 0)
    apart[...] = place_rows(position * slot_count + rank, valid, place.shape[0])
    for k, pair in enumerate(copies):
        for copy in pair:
            copy.wait()
        for copy in (copies[k + 2] if k + 2 < steps else ()):
            copy.start()
        part = slice(k * block, (k + 1) * block)
        product = jnp.dot(tokens[:, part], weight[part, :], preferred_element_type=F32)
        if k == 0:
            total[...] = product
        else:
            total[...] += product
    embed = total[...]
    scale = lax.rsqrt(jnp.sum(embed * embed, axis=1, keepdims=True) + 1e-06)
    near = keep_ref.shape[0]
    unit = (total[:, :early] * scale).astype(BF16)
    send_ref[...] = jnp.dot(apart[near:, :], unit, preferred_element_type=F32).astype(BF16)
    keep_ref[...] = jnp.dot(apart[:near, :], unit, preferred_element_type=F32).astype(BF16)
    late_ref[...] = (total[:, early:] * scale).astype(BF16)


def embed_and_pack(tokens, weight, label_row, valid, owners, slot_count, early):
    rows, depth = tokens.shape
    width = weight.shape[1]
    steps = 4 if depth % 512 == 0 else 1
    width_all = owners * slot_count
    return pl.pallas_call(
        functools.partial(embed_kernel, slot_count, exchange_bits(owners)),
        in_specs=[pl.BlockSpec(memory_space=pltpu.HBM)] * 4,
        out_shape=(
            jax.ShapeDtypeStruct((width_all // 2, early), BF16),
            jax.ShapeDtypeStruct((width_all // 2, early), BF16),
            jax.ShapeDtypeStruct((width_all, rows), BF16),
            jax.ShapeDtypeStruct((rows, width - early), BF16),
            jax.ShapeDtypeStruct((1, rows), jnp.int32),
        ),
        scratch_shapes=[
            pltpu.VMEM((rows, depth), BF16),
            pltpu.VMEM((depth, width), BF16),
            pltpu.VMEM((rows, width), F32),
            pltpu.VMEM((width_all, rows), BF16),
            pltpu.VMEM((1, rows), jnp.int32),
            pltpu.VMEM((rows,), jnp.int32),
            pltpu.SemaphoreType.DMA((steps,)),
            pltpu.SemaphoreType.DMA((steps,)),
            pltpu.SemaphoreType.DMA((2,)),
        ],
        compiler_params=pltpu.CompilerParams(vmem_limit_bytes=EMBED_VMEM_BYTES),
        cost_estimate=pl.CostEstimate(
            flops=2 * rows * depth * width, bytes_accessed=2 * depth * width + 2 * rows * depth, transcendentals=0
        ),
    )(*(pltpu.with_memory_space_constraint(x, pltpu.HBM) for x in (tokens, weight, label_row, valid)))


def pack_kernel(place_ref, unit_ref, packed_ref):
    packed_ref[...] = jnp.dot(place_ref[...], unit_ref[...], preferred_element_type=F32).astype(BF16)


def pack(place, unit):
    width_all, rows = place.shape
    late = unit.shape[1]
    return pl.pallas_call(
        pack_kernel,
        out_shape=jax.ShapeDtypeStruct((width_all, late), BF16),
        compiler_params=pltpu.CompilerParams(vmem_limit_bytes=PACK_VMEM_BYTES),
        cost_estimate=pl.CostEstimate(
            flops=2 * width_all * rows * late, bytes_accessed=2 * width_all * late, transcendentals=0
        ),
    )(place, unit)


def spread_early(keep, send, owners, slot_count):
    early = keep.shape[1]
    *bits, low, high = exchange_bits(owners)
    left = owners // 2
    held = keep.reshape(1, left, slot_count, early)
    leaving = send.reshape(1, left, slot_count, early)
    for bit in bits:
        arrived = lax.ppermute(leaving, "clus", [(i, i ^ bit) for i in range(owners)])
        both = jnp.concatenate([held, arrived], axis=0)
        left //= 2
        held, leaving = both[:, :left], both[:, left:]
    blocks = [both[:, k] for k in range(4)]
    parts = [blocks[0]]
    for block, mask in ((blocks[2], low), (blocks[1], high), (blocks[3], low | high)):
        parts.append(lax.ppermute(block, "clus", [(i, i ^ mask) for i in range(owners)]))
    return jnp.concatenate(parts, axis=0).reshape(owners * slot_count, early)


def order_kernel(slot_count, bits, relative_ref, members_ref):
    width_all = relative_ref.shape[0]
    member = lax.broadcasted_iota(jnp.int32, (width_all, 1), 0)
    source = member // slot_count
    distance = source ^ lax.axis_index("clus")
    index = jnp.zeros_like(distance)
    for k, bit in enumerate(bits):
        index += jnp.where((distance & bit) > 0, 1 << k, 0)
    wanted = index * slot_count + member - source * slot_count
    held = lax.broadcasted_iota(jnp.int32, (width_all, width_all), 1)
    chosen = jnp.where(held == wanted, 1.0, 0.0).astype(BF16)
    members_ref[...] = jnp.dot(chosen, relative_ref[...], preferred_element_type=F32).astype(BF16)


def order_early(relative, owners, slot_count):
    return pl.pallas_call(
        functools.partial(order_kernel, slot_count, exchange_bits(owners)),
        out_shape=jax.ShapeDtypeStruct(relative.shape, BF16),
        compiler_params=pltpu.CompilerParams(vmem_limit_bytes=VMEM_BYTES),
        cost_estimate=pl.CostEstimate(flops=ORDER_FLOPS, bytes_accessed=4 * relative.size, transcendentals=0),
    )(relative)


def score_kernel(slot_count, half, early_ref, late_ref, message_ref, similar_hbm, gram, sem):
    width_all = early_ref.shape[0]
    transposed = (((1,), (1,)), ((), ()))
    owners, lanes = message_ref.shape
    block = width_all // 2
    copies = []
    nears, sums = [], []
    for b in range(2):
        part = slice(b * block, (b + 1) * block)
        tile = lax.dot_general(early_ref[part, :], early_ref[...], transposed, preferred_element_type=F32)
        tile += lax.dot_general(late_ref[part, :], late_ref[...], transposed, preferred_element_type=F32)
        gram[part, :] = tile
        copy = pltpu.make_async_copy(gram.at[part, :], similar_hbm.at[0, part, :], sem.at[b])
        copy.start()
        copies.append(copy)
        own = lax.broadcasted_iota(jnp.int32, (block, width_all), 0) + b * block
        other = lax.broadcasted_iota(jnp.int32, (block, width_all), 1)
        nears.append(jnp.max(jnp.where(own == other, 0.0, tile), axis=0, keepdims=True))
        sums.append(jnp.sum(tile, axis=0, keepdims=True))
    near = jnp.maximum(nears[0], nears[1])
    total = sums[0] + sums[1]
    square = jnp.maximum(jnp.sum(total, axis=1, keepdims=True), 0.0)
    dist = 1.0 - total * lax.rsqrt(square + 1e-06)
    slot = lax.broadcasted_iota(jnp.int32, (width_all, lanes), 0)
    within = slot - (slot // slot_count) * slot_count
    lane = lax.broadcasted_iota(jnp.int32, (width_all, lanes), 1)
    source = lax.broadcasted_iota(jnp.int32, (owners, width_all), 0) * slot_count
    member = lax.broadcasted_iota(jnp.int32, (owners, width_all), 1)
    mine = (member >= source) & (member < source + slot_count)
    out = jnp.zeros((owners, lanes), F32)
    for values, start in ((near, 0), (dist, half)):
        chosen = jnp.where(lane == within + start, 1.0, 0.0).astype(BF16)
        for piece in split3(jnp.where(mine, values, 0.0)):
            out += jnp.dot(piece, chosen, preferred_element_type=F32)
    message_ref[...] = out
    for copy in copies:
        copy.wait()


def scores(early, late, owners, slot_count, half):
    width_all = early.shape[0]
    return pl.pallas_call(
        functools.partial(score_kernel, slot_count, half),
        out_specs=(pl.BlockSpec(memory_space=pltpu.VMEM), pl.BlockSpec(memory_space=pltpu.HBM)),
        out_shape=(
            jax.ShapeDtypeStruct((owners, 2 * half), F32),
            jax.ShapeDtypeStruct((1, width_all, width_all), F32),
        ),
        scratch_shapes=[pltpu.VMEM((width_all, width_all), F32), pltpu.SemaphoreType.DMA((2,))],
        compiler_params=pltpu.CompilerParams(vmem_limit_bytes=VMEM_BYTES),
    )(early, late)


def fetch_kernel(half, message_ref, label_ref, rank_ref, valid_ref, near_ref, dist_ref):
    owners, lanes = message_ref.shape
    rows = label_ref.shape[1]
    owner = lax.broadcasted_iota(jnp.int32, (owners, rows), 0)
    chosen = jnp.where(owner == label_ref[...], 1.0, 0.0).astype(BF16)
    mine = jnp.zeros((lanes, rows), F32)
    for piece in split3(message_ref[...]):
        mine += lax.dot_general(piece, chosen, (((0,), (0,)), ((), ())), preferred_element_type=F32)
    lane = lax.broadcasted_iota(jnp.int32, (lanes, rows), 0)
    rank = rank_ref[...]
    valid = valid_ref[...].astype(F32)
    near_ref[...] = jnp.sum(jnp.where(lane == rank, mine, 0.0), axis=0) * valid
    dist_ref[...] = jnp.sum(jnp.where(lane == rank + half, mine, 0.0), axis=0) * valid


def fetch(message, label_row, rank_row, valid, half):
    rows = label_row.shape[1]
    return pl.pallas_call(
        functools.partial(fetch_kernel, half),
        out_shape=(jax.ShapeDtypeStruct((rows,), F32),) * 2,
        compiler_params=pltpu.CompilerParams(vmem_limit_bytes=FETCH_VMEM_BYTES),
    )(message, label_row, rank_row, valid)


def per_device(tokens, proj_weight, labels, valid_rows):
    row_count = tokens.shape[0]
    owners = lax.axis_size("clus")
    slot_count = 2 * row_count // owners
    width_all = owners * slot_count
    half = -(-slot_count // 64) * 64
    early = EARLY * proj_weight.shape[1] // 8
    label_row = labels.reshape(1, row_count)
    keep, send, place, unit, rank_row = embed_and_pack(
        tokens, proj_weight, label_row, valid_rows, owners, slot_count, early
    )
    arrived = lax.all_to_all(
        pack(place, unit).reshape(owners, slot_count, -1), "clus", split_axis=0, concat_axis=0, tiled=True
    )
    early_members = order_early(spread_early(keep, send, owners, slot_count), owners, slot_count)
    message, similar = scores(early_members, arrived.reshape(width_all, -1), owners, slot_count, half)
    returned = lax.all_to_all(message, "clus", split_axis=0, concat_axis=0, tiled=True)
    nearest, centre_dist = fetch(returned, label_row, rank_row, valid_rows, half)
    return (similar, nearest, centre_dist)


def solution(mesh):
    return jax.shard_map(
        per_device,
        mesh=mesh,
        in_specs=(
            P(("groups", "clus"), None),
            P(),
            P(("groups", "clus"), None),
            P(("groups", "clus")),
        ),
        out_specs=(P(("groups", "clus"), None, None), P(("groups", "clus")), P(("groups", "clus"))),
        check_vma=False,
    )
```

```python
import functools

import jax
import jax.numpy as jnp
from jax import lax
from jax.experimental import pallas as pl
from jax.experimental.pallas import tpu as pltpu
from jax.sharding import PartitionSpec as P

F32 = jnp.float32
BF16 = jnp.bfloat16
VMEM_BYTES = 48 * 1024 * 1024
EMBED_VMEM_BYTES = 40 * 1024 * 1024
PACK_VMEM_BYTES = 16 * 1024 * 1024
FETCH_VMEM_BYTES = 8 * 1024 * 1024
EARLY = 2
ORDER_FLOPS = 13 * 10**9


def split3(x):
    hi = x.astype(BF16)
    rest = x - hi.astype(F32)
    mid = rest.astype(BF16)
    low = (rest - mid.astype(F32)).astype(BF16)
    return hi, mid, low


def rank_rows(label_row):
    rows = label_row.shape[1]
    label = label_row.astype(F32)
    below = lax.broadcasted_iota(jnp.int32, (rows, rows), 0)
    across = lax.broadcasted_iota(jnp.int32, (rows, rows), 1)
    label_col = jnp.sum(jnp.where(below == across, label, 0.0), axis=1, keepdims=True)
    earlier = (label_col == label) & (below < across)
    return jnp.sum(jnp.where(earlier, 1.0, 0.0), axis=0, keepdims=True).astype(jnp.int32)


def place_rows(slot_row, valid_row, width_all):
    slots = lax.broadcasted_iota(jnp.int32, (width_all, slot_row.shape[1]), 0)
    slot = jnp.where(valid_row > 0, slot_row, -1)
    return jnp.where(slots == slot, 1.0, 0.0).astype(BF16)


def exchange_bits(owners):
    middle = []
    bit = 1
    while bit < owners // 8:
        middle.append(bit)
        bit *= 2
    return [owners // 2] + middle + [owners // 8, owners // 4]


def embed_kernel(
    slot_count, bits, tokens_hbm, weight_hbm, label_hbm, valid_hbm, keep_ref, send_ref, slot_ref, late_ref, rank_ref,
    tokens, weight, total, apart, label_ref, valid_ref, token_sem, weight_sem, small_sem,
):
    steps = token_sem.shape[0]
    block = tokens.shape[1] // steps
    early = keep_ref.shape[1]
    small = (
        pltpu.make_async_copy(label_hbm, label_ref, small_sem.at[0]),
        pltpu.make_async_copy(valid_hbm, valid_ref, small_sem.at[1]),
    )
    for copy in small:
        copy.start()
    copies = []
    for k in range(steps):
        part = slice(k * block, (k + 1) * block)
        copies.append((
            pltpu.make_async_copy(tokens_hbm.at[:, part], tokens.at[:, part], token_sem.at[k]),
            pltpu.make_async_copy(weight_hbm.at[part, :], weight.at[part, :], weight_sem.at[k]),
        ))
    for pair in copies[:2]:
        for copy in pair:
            copy.start()
    for copy in small:
        copy.wait()
    label = label_ref[...]
    valid = valid_ref[...].reshape(label.shape)
    rank = rank_rows(label)
    rank_ref[...] = rank
    slot_ref[...] = jnp.where(valid > 0, label * slot_count + rank, -1)
    distance = label ^ lax.axis_index("clus")
    position = jnp.zeros_like(label)
    for k, bit in enumerate(bits):
        position += jnp.where((distance & bit) > 0, 1 << (len(bits) - 1 - k), 0)
    apart[...] = place_rows(position * slot_count + rank, valid, apart.shape[0])
    for k, pair in enumerate(copies):
        for copy in pair:
            copy.wait()
        for copy in (copies[k + 2] if k + 2 < steps else ()):
            copy.start()
        part = slice(k * block, (k + 1) * block)
        product = jnp.dot(tokens[:, part], weight[part, :], preferred_element_type=F32)
        if k == 0:
            total[...] = product
        else:
            total[...] += product
    embed = total[...]
    scale = lax.rsqrt(jnp.sum(embed * embed, axis=1, keepdims=True) + 1e-06)
    near = keep_ref.shape[0]
    unit = (total[:, :early] * scale).astype(BF16)
    send_ref[...] = jnp.dot(apart[near:, :], unit, preferred_element_type=F32).astype(BF16)
    keep_ref[...] = jnp.dot(apart[:near, :], unit, preferred_element_type=F32).astype(BF16)
    late_ref[...] = (total[:, early:] * scale).astype(BF16)


def embed_and_pack(tokens, weight, label_row, valid, owners, slot_count, early):
    rows, depth = tokens.shape
    width = weight.shape[1]
    steps = 4 if depth % 512 == 0 else 1
    width_all = owners * slot_count
    return pl.pallas_call(
        functools.partial(embed_kernel, slot_count, exchange_bits(owners)),
        in_specs=[pl.BlockSpec(memory_space=pltpu.HBM)] * 4,
        out_shape=(
            jax.ShapeDtypeStruct((width_all // 2, early), BF16),
            jax.ShapeDtypeStruct((width_all // 2, early), BF16),
            jax.ShapeDtypeStruct((1, rows), jnp.int32),
            jax.ShapeDtypeStruct((rows, width - early), BF16),
            jax.ShapeDtypeStruct((1, rows), jnp.int32),
        ),
        scratch_shapes=[
            pltpu.VMEM((rows, depth), BF16),
            pltpu.VMEM((depth, width), BF16),
            pltpu.VMEM((rows, width), F32),
            pltpu.VMEM((width_all, rows), BF16),
            pltpu.VMEM((1, rows), jnp.int32),
            pltpu.VMEM((rows,), jnp.int32),
            pltpu.SemaphoreType.DMA((steps,)),
            pltpu.SemaphoreType.DMA((steps,)),
            pltpu.SemaphoreType.DMA((2,)),
        ],
        compiler_params=pltpu.CompilerParams(vmem_limit_bytes=EMBED_VMEM_BYTES),
        cost_estimate=pl.CostEstimate(
            flops=2 * rows * depth * width, bytes_accessed=2 * depth * width + 2 * rows * depth, transcendentals=0
        ),
    )(*(pltpu.with_memory_space_constraint(x, pltpu.HBM) for x in (tokens, weight, label_row, valid)))


def pack_kernel(slot_ref, unit_ref, packed_ref):
    slot = slot_ref[...]
    place = place_rows(slot, slot + 1, packed_ref.shape[0])
    packed_ref[...] = jnp.dot(place, unit_ref[...], preferred_element_type=F32).astype(BF16)


def pack(slot_row, unit, width_all):
    rows, late = unit.shape
    return pl.pallas_call(
        pack_kernel,
        out_shape=jax.ShapeDtypeStruct((width_all, late), BF16),
        compiler_params=pltpu.CompilerParams(vmem_limit_bytes=PACK_VMEM_BYTES),
        cost_estimate=pl.CostEstimate(
            flops=2 * width_all * rows * late, bytes_accessed=2 * width_all * late, transcendentals=0
        ),
    )(slot_row, unit)


def spread_early(keep, send, owners, slot_count):
    early = keep.shape[1]
    *bits, low, high = exchange_bits(owners)
    left = owners // 2
    held = keep.reshape(1, left, slot_count, early)
    leaving = send.reshape(1, left, slot_count, early)
    for bit in bits:
        arrived = lax.ppermute(leaving, "clus", [(i, i ^ bit) for i in range(owners)])
        both = jnp.concatenate([held, arrived], axis=0)
        left //= 2
        held, leaving = both[:, :left], both[:, left:]
    blocks = [both[:, k] for k in range(4)]
    parts = [blocks[0]]
    for block, mask in ((blocks[2], low), (blocks[1], high), (blocks[3], low | high)):
        parts.append(lax.ppermute(block, "clus", [(i, i ^ mask) for i in range(owners)]))
    return jnp.concatenate(parts, axis=0).reshape(owners * slot_count, early)


def order_kernel(slot_count, bits, relative_ref, gram_ref):
    width_all = relative_ref.shape[0]
    member = lax.broadcasted_iota(jnp.int32, (width_all, 1), 0)
    source = member // slot_count
    distance = source ^ lax.axis_index("clus")
    index = jnp.zeros_like(distance)
    for k, bit in enumerate(bits):
        index += jnp.where((distance & bit) > 0, 1 << k, 0)
    wanted = index * slot_count + member - source * slot_count
    held = lax.broadcasted_iota(jnp.int32, (width_all, width_all), 1)
    chosen = jnp.where(held == wanted, 1.0, 0.0).astype(BF16)
    members = jnp.dot(chosen, relative_ref[...], preferred_element_type=F32).astype(BF16)
    gram_ref[...] = lax.dot_general(members, members, (((1,), (1,)), ((), ())), preferred_element_type=F32)


def order_early(relative, owners, slot_count):
    return pl.pallas_call(
        functools.partial(order_kernel, slot_count, exchange_bits(owners)),
        out_shape=jax.ShapeDtypeStruct((relative.shape[0],) * 2, F32),
        compiler_params=pltpu.CompilerParams(vmem_limit_bytes=VMEM_BYTES),
        cost_estimate=pl.CostEstimate(flops=ORDER_FLOPS, bytes_accessed=4 * relative.size, transcendentals=0),
    )(relative)


def score_kernel(slot_count, half, early_ref, late_ref, message_ref, similar_hbm, gram, sem):
    width_all = early_ref.shape[0]
    transposed = (((1,), (1,)), ((), ()))
    owners, lanes = message_ref.shape
    block = width_all // 2
    copies = []
    nears, sums = [], []
    for b in range(2):
        part = slice(b * block, (b + 1) * block)
        tile = lax.dot_general(late_ref[part, :], late_ref[...], transposed, preferred_element_type=F32)
        tile += early_ref[part, :]
        gram[part, :] = tile
        copy = pltpu.make_async_copy(gram.at[part, :], similar_hbm.at[0, part, :], sem.at[b])
        copy.start()
        copies.append(copy)
        own = lax.broadcasted_iota(jnp.int32, (block, width_all), 0) + b * block
        other = lax.broadcasted_iota(jnp.int32, (block, width_all), 1)
        nears.append(jnp.max(jnp.where(own == other, 0.0, tile), axis=0, keepdims=True))
        sums.append(jnp.sum(tile, axis=0, keepdims=True))
    near = jnp.maximum(nears[0], nears[1])
    total = sums[0] + sums[1]
    square = jnp.maximum(jnp.sum(total, axis=1, keepdims=True), 0.0)
    dist = 1.0 - total * lax.rsqrt(square + 1e-06)
    slot = lax.broadcasted_iota(jnp.int32, (width_all, lanes), 0)
    within = slot - (slot // slot_count) * slot_count
    lane = lax.broadcasted_iota(jnp.int32, (width_all, lanes), 1)
    source = lax.broadcasted_iota(jnp.int32, (owners, width_all), 0) * slot_count
    member = lax.broadcasted_iota(jnp.int32, (owners, width_all), 1)
    mine = (member >= source) & (member < source + slot_count)
    out = jnp.zeros((owners, lanes), F32)
    for values, start in ((near, 0), (dist, half)):
        chosen = jnp.where(lane == within + start, 1.0, 0.0).astype(BF16)
        for piece in split3(jnp.where(mine, values, 0.0)):
            out += jnp.dot(piece, chosen, preferred_element_type=F32)
    message_ref[...] = out
    for copy in copies:
        copy.wait()


def scores(early, late, owners, slot_count, half):
    width_all = early.shape[0]
    return pl.pallas_call(
        functools.partial(score_kernel, slot_count, half),
        out_specs=(pl.BlockSpec(memory_space=pltpu.VMEM), pl.BlockSpec(memory_space=pltpu.HBM)),
        out_shape=(
            jax.ShapeDtypeStruct((owners, 2 * half), F32),
            jax.ShapeDtypeStruct((1, width_all, width_all), F32),
        ),
        scratch_shapes=[pltpu.VMEM((width_all, width_all), F32), pltpu.SemaphoreType.DMA((2,))],
        compiler_params=pltpu.CompilerParams(vmem_limit_bytes=VMEM_BYTES),
    )(early, late)


def fetch_kernel(half, message_ref, label_ref, rank_ref, valid_ref, near_ref, dist_ref):
    owners, lanes = message_ref.shape
    rows = label_ref.shape[1]
    owner = lax.broadcasted_iota(jnp.int32, (owners, rows), 0)
    chosen = jnp.where(owner == label_ref[...], 1.0, 0.0).astype(BF16)
    mine = jnp.zeros((lanes, rows), F32)
    for piece in split3(message_ref[...]):
        mine += lax.dot_general(piece, chosen, (((0,), (0,)), ((), ())), preferred_element_type=F32)
    lane = lax.broadcasted_iota(jnp.int32, (lanes, rows), 0)
    rank = rank_ref[...]
    valid = valid_ref[...].astype(F32)
    near_ref[...] = jnp.sum(jnp.where(lane == rank, mine, 0.0), axis=0) * valid
    dist_ref[...] = jnp.sum(jnp.where(lane == rank + half, mine, 0.0), axis=0) * valid


def fetch(message, label_row, rank_row, valid, half):
    rows = label_row.shape[1]
    return pl.pallas_call(
        functools.partial(fetch_kernel, half),
        out_shape=(jax.ShapeDtypeStruct((rows,), F32),) * 2,
        compiler_params=pltpu.CompilerParams(vmem_limit_bytes=FETCH_VMEM_BYTES),
    )(message, label_row, rank_row, valid)


def per_device(tokens, proj_weight, labels, valid_rows):
    row_count = tokens.shape[0]
    owners = lax.axis_size("clus")
    slot_count = 2 * row_count // owners
    width_all = owners * slot_count
    half = -(-slot_count // 64) * 64
    early = EARLY * proj_weight.shape[1] // 8
    label_row = labels.reshape(1, row_count)
    keep, send, slot_row, unit, rank_row = embed_and_pack(
        tokens, proj_weight, label_row, valid_rows, owners, slot_count, early
    )
    arrived = lax.all_to_all(
        pack(slot_row, unit, width_all).reshape(owners, slot_count, -1), "clus", split_axis=0, concat_axis=0, tiled=True
    )
    early_gram = order_early(spread_early(keep, send, owners, slot_count), owners, slot_count)
    message, similar = scores(early_gram, arrived.reshape(width_all, -1), owners, slot_count, half)
    returned = lax.all_to_all(message, "clus", split_axis=0, concat_axis=0, tiled=True)
    nearest, centre_dist = fetch(returned, label_row, rank_row, valid_rows, half)
    return (similar, nearest, centre_dist)


def solution(mesh):
    return jax.shard_map(
        per_device,
        mesh=mesh,
        in_specs=(
            P(("groups", "clus"), None),
            P(),
            P(("groups", "clus"), None),
            P(("groups", "clus")),
        ),
        out_specs=(P(("groups", "clus"), None, None), P(("groups", "clus")), P(("groups", "clus"))),
        check_vma=False,
    )
```

```python
import functools

import jax
import jax.numpy as jnp
from jax import lax
from jax.experimental import pallas as pl
from jax.experimental.pallas import tpu as pltpu
from jax.sharding import PartitionSpec as P

F32 = jnp.float32
BF16 = jnp.bfloat16
VMEM_BYTES = 48 * 1024 * 1024
EMBED_VMEM_BYTES = 40 * 1024 * 1024
PACK_VMEM_BYTES = 16 * 1024 * 1024
FETCH_VMEM_BYTES = 8 * 1024 * 1024
PARTS = 32
EDGES = (0, 8, 18, 26, 32)
EARLY = 2
ORDER_FLOPS = 13 * 10**9


def split3(x):
    hi = x.astype(BF16)
    rest = x - hi.astype(F32)
    mid = rest.astype(BF16)
    low = (rest - mid.astype(F32)).astype(BF16)
    return hi, mid, low


def rank_rows(label_row):
    rows = label_row.shape[1]
    label = label_row.astype(F32)
    below = lax.broadcasted_iota(jnp.int32, (rows, rows), 0)
    across = lax.broadcasted_iota(jnp.int32, (rows, rows), 1)
    label_col = jnp.sum(jnp.where(below == across, label, 0.0), axis=1, keepdims=True)
    earlier = (label_col == label) & (below < across)
    return jnp.sum(jnp.where(earlier, 1.0, 0.0), axis=0, keepdims=True).astype(jnp.int32)


def place_rows(slot_row, valid_row, width_all):
    slots = lax.broadcasted_iota(jnp.int32, (width_all, slot_row.shape[1]), 0)
    slot = jnp.where(valid_row > 0, slot_row, -1)
    return jnp.where(slots == slot, 1.0, 0.0).astype(BF16)


def exchange_bits(owners):
    middle = []
    bit = 1
    while bit < owners // 8:
        middle.append(bit)
        bit *= 2
    return [owners // 2] + middle + [owners // 8, owners // 4]


def embed_kernel(
    slot_count, bits, tokens_hbm, weight_hbm, label_hbm, valid_hbm, keep_ref, send_ref, slot_ref, late_ref, rank_ref,
    tokens, weight, total, apart, label_ref, valid_ref, token_sem, weight_sem, small_sem,
):
    steps = token_sem.shape[0]
    depth = tokens.shape[1]
    edges = [depth * part // PARTS for part in EDGES] if steps == len(EDGES) - 1 else [0, depth]
    early = keep_ref.shape[1]
    small = (
        pltpu.make_async_copy(label_hbm, label_ref, small_sem.at[0]),
        pltpu.make_async_copy(valid_hbm, valid_ref, small_sem.at[1]),
    )
    for copy in small:
        copy.start()
    copies = []
    for k in range(steps):
        part = slice(edges[k], edges[k + 1])
        copies.append((
            pltpu.make_async_copy(tokens_hbm.at[:, part], tokens.at[:, part], token_sem.at[k]),
            pltpu.make_async_copy(weight_hbm.at[part, :], weight.at[part, :], weight_sem.at[k]),
        ))
    for pair in copies[:2]:
        for copy in pair:
            copy.start()
    for copy in small:
        copy.wait()
    label = label_ref[...]
    valid = valid_ref[...].reshape(label.shape)
    rank = rank_rows(label)
    rank_ref[...] = rank
    slot_ref[...] = jnp.where(valid > 0, label * slot_count + rank, -1)
    distance = label ^ lax.axis_index("clus")
    position = jnp.zeros_like(label)
    for k, bit in enumerate(bits):
        position += jnp.where((distance & bit) > 0, 1 << (len(bits) - 1 - k), 0)
    apart[...] = place_rows(position * slot_count + rank, valid, apart.shape[0])
    for k, pair in enumerate(copies):
        for copy in pair:
            copy.wait()
        for copy in (copies[k + 2] if k + 2 < steps else ()):
            copy.start()
        part = slice(edges[k], edges[k + 1])
        product = jnp.dot(tokens[:, part], weight[part, :], preferred_element_type=F32)
        if k == 0:
            total[...] = product
        else:
            total[...] += product
    embed = total[...]
    scale = lax.rsqrt(jnp.sum(embed * embed, axis=1, keepdims=True) + 1e-06)
    near = keep_ref.shape[0]
    unit = (total[:, :early] * scale).astype(BF16)
    send_ref[...] = jnp.dot(apart[near:, :], unit, preferred_element_type=F32).astype(BF16)
    keep_ref[...] = jnp.dot(apart[:near, :], unit, preferred_element_type=F32).astype(BF16)
    late_ref[...] = (total[:, early:] * scale).astype(BF16)


def embed_and_pack(tokens, weight, label_row, valid, owners, slot_count, early):
    rows, depth = tokens.shape
    width = weight.shape[1]
    steps = len(EDGES) - 1 if depth % (128 * PARTS) == 0 else 1
    width_all = owners * slot_count
    return pl.pallas_call(
        functools.partial(embed_kernel, slot_count, exchange_bits(owners)),
        in_specs=[pl.BlockSpec(memory_space=pltpu.HBM)] * 4,
        out_shape=(
            jax.ShapeDtypeStruct((width_all // 2, early), BF16),
            jax.ShapeDtypeStruct((width_all // 2, early), BF16),
            jax.ShapeDtypeStruct((1, rows), jnp.int32),
            jax.ShapeDtypeStruct((rows, width - early), BF16),
            jax.ShapeDtypeStruct((1, rows), jnp.int32),
        ),
        scratch_shapes=[
            pltpu.VMEM((rows, depth), BF16),
            pltpu.VMEM((depth, width), BF16),
            pltpu.VMEM((rows, width), F32),
            pltpu.VMEM((width_all, rows), BF16),
            pltpu.VMEM((1, rows), jnp.int32),
            pltpu.VMEM((rows,), jnp.int32),
            pltpu.SemaphoreType.DMA((steps,)),
            pltpu.SemaphoreType.DMA((steps,)),
            pltpu.SemaphoreType.DMA((2,)),
        ],
        compiler_params=pltpu.CompilerParams(vmem_limit_bytes=EMBED_VMEM_BYTES),
        cost_estimate=pl.CostEstimate(
            flops=2 * rows * depth * width, bytes_accessed=2 * depth * width + 2 * rows * depth, transcendentals=0
        ),
    )(*(pltpu.with_memory_space_constraint(x, pltpu.HBM) for x in (tokens, weight, label_row, valid)))


def pack_kernel(slot_ref, unit_ref, packed_ref):
    slot = slot_ref[...]
    place = place_rows(slot, slot + 1, packed_ref.shape[0])
    packed_ref[...] = jnp.dot(place, unit_ref[...], preferred_element_type=F32).astype(BF16)


def pack(slot_row, unit, width_all):
    rows, late = unit.shape
    return pl.pallas_call(
        pack_kernel,
        out_shape=jax.ShapeDtypeStruct((width_all, late), BF16),
        compiler_params=pltpu.CompilerParams(vmem_limit_bytes=PACK_VMEM_BYTES),
        cost_estimate=pl.CostEstimate(
            flops=2 * width_all * rows * late, bytes_accessed=2 * width_all * late, transcendentals=0
        ),
    )(slot_row, unit)


def spread_early(keep, send, owners, slot_count):
    early = keep.shape[1]
    *bits, low, high = exchange_bits(owners)
    left = owners // 2
    held = keep.reshape(1, left, slot_count, early)
    leaving = send.reshape(1, left, slot_count, early)
    for bit in bits:
        arrived = lax.ppermute(leaving, "clus", [(i, i ^ bit) for i in range(owners)])
        both = jnp.concatenate([held, arrived], axis=0)
        left //= 2
        held, leaving = both[:, :left], both[:, left:]
    blocks = [both[:, k] for k in range(4)]
    parts = [blocks[0]]
    for block, mask in ((blocks[2], low), (blocks[1], high), (blocks[3], low | high)):
        parts.append(lax.ppermute(block, "clus", [(i, i ^ mask) for i in range(owners)]))
    return jnp.concatenate(parts, axis=0).reshape(owners * slot_count, early)


def order_kernel(slot_count, bits, relative_ref, gram_ref):
    width_all = relative_ref.shape[0]
    member = lax.broadcasted_iota(jnp.int32, (width_all, 1), 0)
    source = member // slot_count
    distance = source ^ lax.axis_index("clus")
    index = jnp.zeros_like(distance)
    for k, bit in enumerate(bits):
        index += jnp.where((distance & bit) > 0, 1 << k, 0)
    wanted = index * slot_count + member - source * slot_count
    held = lax.broadcasted_iota(jnp.int32, (width_all, width_all), 1)
    chosen = jnp.where(held == wanted, 1.0, 0.0).astype(BF16)
    members = jnp.dot(chosen, relative_ref[...], preferred_element_type=F32).astype(BF16)
    gram_ref[...] = lax.dot_general(members, members, (((1,), (1,)), ((), ())), preferred_element_type=F32)


def order_early(relative, owners, slot_count):
    return pl.pallas_call(
        functools.partial(order_kernel, slot_count, exchange_bits(owners)),
        out_shape=jax.ShapeDtypeStruct((relative.shape[0],) * 2, F32),
        compiler_params=pltpu.CompilerParams(vmem_limit_bytes=VMEM_BYTES),
        cost_estimate=pl.CostEstimate(flops=ORDER_FLOPS, bytes_accessed=4 * relative.size, transcendentals=0),
    )(relative)


def score_kernel(slot_count, half, early_ref, late_ref, message_ref, similar_hbm, gram, sem):
    width_all = early_ref.shape[0]
    transposed = (((1,), (1,)), ((), ()))
    owners, lanes = message_ref.shape
    block = width_all // 2
    copies = []
    nears, sums = [], []
    for b in range(2):
        part = slice(b * block, (b + 1) * block)
        tile = lax.dot_general(late_ref[part, :], late_ref[...], transposed, preferred_element_type=F32)
        tile += early_ref[part, :]
        gram[part, :] = tile
        copy = pltpu.make_async_copy(gram.at[part, :], similar_hbm.at[0, part, :], sem.at[b])
        copy.start()
        copies.append(copy)
        own = lax.broadcasted_iota(jnp.int32, (block, width_all), 0) + b * block
        other = lax.broadcasted_iota(jnp.int32, (block, width_all), 1)
        nears.append(jnp.max(jnp.where(own == other, 0.0, tile), axis=0, keepdims=True))
        sums.append(jnp.sum(tile, axis=0, keepdims=True))
    near = jnp.maximum(nears[0], nears[1])
    total = sums[0] + sums[1]
    square = jnp.maximum(jnp.sum(total, axis=1, keepdims=True), 0.0)
    dist = 1.0 - total * lax.rsqrt(square + 1e-06)
    slot = lax.broadcasted_iota(jnp.int32, (width_all, lanes), 0)
    within = slot - (slot // slot_count) * slot_count
    lane = lax.broadcasted_iota(jnp.int32, (width_all, lanes), 1)
    source = lax.broadcasted_iota(jnp.int32, (owners, width_all), 0) * slot_count
    member = lax.broadcasted_iota(jnp.int32, (owners, width_all), 1)
    mine = (member >= source) & (member < source + slot_count)
    out = jnp.zeros((owners, lanes), F32)
    for values, start in ((near, 0), (dist, half)):
        chosen = jnp.where(lane == within + start, 1.0, 0.0).astype(BF16)
        for piece in split3(jnp.where(mine, values, 0.0)):
            out += jnp.dot(piece, chosen, preferred_element_type=F32)
    message_ref[...] = out
    for copy in copies:
        copy.wait()


def scores(early, late, owners, slot_count, half):
    width_all = early.shape[0]
    return pl.pallas_call(
        functools.partial(score_kernel, slot_count, half),
        out_specs=(pl.BlockSpec(memory_space=pltpu.VMEM), pl.BlockSpec(memory_space=pltpu.HBM)),
        out_shape=(
            jax.ShapeDtypeStruct((owners, 2 * half), F32),
            jax.ShapeDtypeStruct((1, width_all, width_all), F32),
        ),
        scratch_shapes=[pltpu.VMEM((width_all, width_all), F32), pltpu.SemaphoreType.DMA((2,))],
        compiler_params=pltpu.CompilerParams(vmem_limit_bytes=VMEM_BYTES),
    )(early, late)


def fetch_kernel(half, message_ref, label_ref, rank_ref, valid_ref, near_ref, dist_ref):
    owners, lanes = message_ref.shape
    rows = label_ref.shape[1]
    owner = lax.broadcasted_iota(jnp.int32, (owners, rows), 0)
    chosen = jnp.where(owner == label_ref[...], 1.0, 0.0).astype(BF16)
    mine = jnp.zeros((lanes, rows), F32)
    for piece in split3(message_ref[...]):
        mine += lax.dot_general(piece, chosen, (((0,), (0,)), ((), ())), preferred_element_type=F32)
    lane = lax.broadcasted_iota(jnp.int32, (lanes, rows), 0)
    rank = rank_ref[...]
    valid = valid_ref[...].astype(F32)
    near_ref[...] = jnp.sum(jnp.where(lane == rank, mine, 0.0), axis=0) * valid
    dist_ref[...] = jnp.sum(jnp.where(lane == rank + half, mine, 0.0), axis=0) * valid


def fetch(message, label_row, rank_row, valid, half):
    rows = label_row.shape[1]
    return pl.pallas_call(
        functools.partial(fetch_kernel, half),
        out_shape=(jax.ShapeDtypeStruct((rows,), F32),) * 2,
        compiler_params=pltpu.CompilerParams(vmem_limit_bytes=FETCH_VMEM_BYTES),
    )(message, label_row, rank_row, valid)


def per_device(tokens, proj_weight, labels, valid_rows):
    row_count = tokens.shape[0]
    owners = lax.axis_size("clus")
    slot_count = 2 * row_count // owners
    width_all = owners * slot_count
    half = -(-slot_count // 64) * 64
    early = EARLY * proj_weight.shape[1] // 8
    label_row = labels.reshape(1, row_count)
    keep, send, slot_row, unit, rank_row = embed_and_pack(
        tokens, proj_weight, label_row, valid_rows, owners, slot_count, early
    )
    arrived = lax.all_to_all(
        pack(slot_row, unit, width_all).reshape(owners, slot_count, -1), "clus", split_axis=0, concat_axis=0, tiled=True
    )
    early_gram = order_early(spread_early(keep, send, owners, slot_count), owners, slot_count)
    message, similar = scores(early_gram, arrived.reshape(width_all, -1), owners, slot_count, half)
    returned = lax.all_to_all(message, "clus", split_axis=0, concat_axis=0, tiled=True)
    nearest, centre_dist = fetch(returned, label_row, rank_row, valid_rows, half)
    return (similar, nearest, centre_dist)


def solution(mesh):
    return jax.shard_map(
        per_device,
        mesh=mesh,
        in_specs=(
            P(("groups", "clus"), None),
            P(),
            P(("groups", "clus"), None),
            P(("groups", "clus")),
        ),
        out_specs=(P(("groups", "clus"), None, None), P(("groups", "clus")), P(("groups", "clus"))),
        check_vma=False,
    )
```

```python
import functools

import jax
import jax.numpy as jnp
from jax import lax
from jax.experimental import pallas as pl
from jax.experimental.pallas import tpu as pltpu
from jax.sharding import PartitionSpec as P

F32 = jnp.float32
BF16 = jnp.bfloat16
VMEM_BYTES = 48 * 1024 * 1024
EMBED_VMEM_BYTES = 40 * 1024 * 1024
PACK_VMEM_BYTES = 16 * 1024 * 1024
FETCH_VMEM_BYTES = 8 * 1024 * 1024
PARTS = 32
EDGES = (0, 8, 18, 26, 32)
EARLY = 2
ORDER_FLOPS = 13 * 10**9


def split3(x):
    hi = x.astype(BF16)
    rest = x - hi.astype(F32)
    mid = rest.astype(BF16)
    low = (rest - mid.astype(F32)).astype(BF16)
    return hi, mid, low


def rank_rows(label_row):
    rows = label_row.shape[1]
    label = label_row.astype(F32)
    below = lax.broadcasted_iota(jnp.int32, (rows, rows), 0)
    across = lax.broadcasted_iota(jnp.int32, (rows, rows), 1)
    label_col = jnp.sum(jnp.where(below == across, label, 0.0), axis=1, keepdims=True)
    earlier = (label_col == label) & (below < across)
    return jnp.sum(jnp.where(earlier, 1.0, 0.0), axis=0, keepdims=True).astype(jnp.int32)


def place_rows(slot_row, valid_row, width_all):
    slots = lax.broadcasted_iota(jnp.int32, (width_all, slot_row.shape[1]), 0)
    slot = jnp.where(valid_row > 0, slot_row, -1)
    return jnp.where(slots == slot, 1.0, 0.0).astype(BF16)


def exchange_bits(owners):
    middle = []
    bit = 1
    while bit < owners // 8:
        middle.append(bit)
        bit *= 2
    return [owners // 2] + middle + [owners // 8, owners // 4]


def embed_kernel(
    slot_count, bits, tokens_hbm, weight_hbm, label_hbm, valid_hbm, keep_ref, send_ref, slot_ref, total, scale_ref, rank_ref,
    tokens, weight, apart, label_ref, valid_ref, token_sem, weight_sem, small_sem,
):
    steps = token_sem.shape[0]
    depth = tokens.shape[1]
    edges = [depth * part // PARTS for part in EDGES] if steps == len(EDGES) - 1 else [0, depth]
    early = keep_ref.shape[1]
    small = (
        pltpu.make_async_copy(label_hbm, label_ref, small_sem.at[0]),
        pltpu.make_async_copy(valid_hbm, valid_ref, small_sem.at[1]),
    )
    for copy in small:
        copy.start()
    copies = []
    for k in range(steps):
        part = slice(edges[k], edges[k + 1])
        copies.append((
            pltpu.make_async_copy(tokens_hbm.at[:, part], tokens.at[:, part], token_sem.at[k]),
            pltpu.make_async_copy(weight_hbm.at[part, :], weight.at[part, :], weight_sem.at[k]),
        ))
    for pair in copies[:2]:
        for copy in pair:
            copy.start()
    for copy in small:
        copy.wait()
    label = label_ref[...]
    valid = valid_ref[...].reshape(label.shape)
    rank = rank_rows(label)
    rank_ref[...] = rank
    slot_ref[...] = jnp.where(valid > 0, label * slot_count + rank, -1)
    distance = label ^ lax.axis_index("clus")
    position = jnp.zeros_like(label)
    for k, bit in enumerate(bits):
        position += jnp.where((distance & bit) > 0, 1 << (len(bits) - 1 - k), 0)
    apart[...] = place_rows(position * slot_count + rank, valid, apart.shape[0])
    for k, pair in enumerate(copies):
        for copy in pair:
            copy.wait()
        for copy in (copies[k + 2] if k + 2 < steps else ()):
            copy.start()
        part = slice(edges[k], edges[k + 1])
        product = jnp.dot(tokens[:, part], weight[part, :], preferred_element_type=F32)
        if k == 0:
            total[...] = product
        else:
            total[...] += product
    embed = total[...]
    scale = lax.rsqrt(jnp.sum(embed * embed, axis=1, keepdims=True) + 1e-06)
    near = keep_ref.shape[0]
    unit = (total[:, :early] * scale).astype(BF16)
    send_ref[...] = jnp.dot(apart[near:, :], unit, preferred_element_type=F32).astype(BF16)
    keep_ref[...] = jnp.dot(apart[:near, :], unit, preferred_element_type=F32).astype(BF16)
    scale_ref[...] = scale


def embed_and_pack(tokens, weight, label_row, valid, owners, slot_count, early):
    rows, depth = tokens.shape
    width = weight.shape[1]
    steps = len(EDGES) - 1 if depth % (128 * PARTS) == 0 else 1
    width_all = owners * slot_count
    return pl.pallas_call(
        functools.partial(embed_kernel, slot_count, exchange_bits(owners)),
        in_specs=[pl.BlockSpec(memory_space=pltpu.HBM)] * 4,
        out_shape=(
            jax.ShapeDtypeStruct((width_all // 2, early), BF16),
            jax.ShapeDtypeStruct((width_all // 2, early), BF16),
            jax.ShapeDtypeStruct((1, rows), jnp.int32),
            jax.ShapeDtypeStruct((rows, width), F32),
            jax.ShapeDtypeStruct((rows, 1), F32),
            jax.ShapeDtypeStruct((1, rows), jnp.int32),
        ),
        scratch_shapes=[
            pltpu.VMEM((rows, depth), BF16),
            pltpu.VMEM((depth, width), BF16),
            pltpu.VMEM((width_all, rows), BF16),
            pltpu.VMEM((1, rows), jnp.int32),
            pltpu.VMEM((rows,), jnp.int32),
            pltpu.SemaphoreType.DMA((steps,)),
            pltpu.SemaphoreType.DMA((steps,)),
            pltpu.SemaphoreType.DMA((2,)),
        ],
        compiler_params=pltpu.CompilerParams(vmem_limit_bytes=EMBED_VMEM_BYTES),
        cost_estimate=pl.CostEstimate(
            flops=2 * rows * depth * width, bytes_accessed=2 * depth * width + 2 * rows * depth, transcendentals=0
        ),
    )(*(pltpu.with_memory_space_constraint(x, pltpu.HBM) for x in (tokens, weight, label_row, valid)))


def pack_kernel(slot_ref, total_ref, scale_ref, packed_ref):
    early = total_ref.shape[1] - packed_ref.shape[1]
    unit = (total_ref[:, early:] * scale_ref[...]).astype(BF16)
    slot = slot_ref[...]
    place = place_rows(slot, slot + 1, packed_ref.shape[0])
    packed_ref[...] = jnp.dot(place, unit, preferred_element_type=F32).astype(BF16)


def pack(slot_row, total, scale, width_all, early):
    rows = total.shape[0]
    late = total.shape[1] - early
    return pl.pallas_call(
        pack_kernel,
        out_shape=jax.ShapeDtypeStruct((width_all, late), BF16),
        compiler_params=pltpu.CompilerParams(vmem_limit_bytes=PACK_VMEM_BYTES),
        cost_estimate=pl.CostEstimate(
            flops=2 * width_all * rows * late, bytes_accessed=2 * width_all * late, transcendentals=0
        ),
    )(slot_row, total, scale)


def spread_early(keep, send, owners, slot_count):
    early = keep.shape[1]
    *bits, low, high = exchange_bits(owners)
    left = owners // 2
    held = keep.reshape(1, left, slot_count, early)
    leaving = send.reshape(1, left, slot_count, early)
    for bit in bits:
        arrived = lax.ppermute(leaving, "clus", [(i, i ^ bit) for i in range(owners)])
        both = jnp.concatenate([held, arrived], axis=0)
        left //= 2
        held, leaving = both[:, :left], both[:, left:]
    blocks = [both[:, k] for k in range(4)]
    parts = [blocks[0]]
    for block, mask in ((blocks[2], low), (blocks[1], high), (blocks[3], low | high)):
        parts.append(lax.ppermute(block, "clus", [(i, i ^ mask) for i in range(owners)]))
    return jnp.concatenate(parts, axis=0).reshape(owners * slot_count, early)


def order_kernel(slot_count, bits, relative_ref, gram_ref):
    width_all = relative_ref.shape[0]
    member = lax.broadcasted_iota(jnp.int32, (width_all, 1), 0)
    source = member // slot_count
    distance = source ^ lax.axis_index("clus")
    index = jnp.zeros_like(distance)
    for k, bit in enumerate(bits):
        index += jnp.where((distance & bit) > 0, 1 << k, 0)
    wanted = index * slot_count + member - source * slot_count
    held = lax.broadcasted_iota(jnp.int32, (width_all, width_all), 1)
    chosen = jnp.where(held == wanted, 1.0, 0.0).astype(BF16)
    members = jnp.dot(chosen, relative_ref[...], preferred_element_type=F32).astype(BF16)
    gram_ref[...] = lax.dot_general(members, members, (((1,), (1,)), ((), ())), preferred_element_type=F32)


def order_early(relative, owners, slot_count):
    return pl.pallas_call(
        functools.partial(order_kernel, slot_count, exchange_bits(owners)),
        out_shape=jax.ShapeDtypeStruct((relative.shape[0],) * 2, F32),
        compiler_params=pltpu.CompilerParams(vmem_limit_bytes=VMEM_BYTES),
        cost_estimate=pl.CostEstimate(flops=ORDER_FLOPS, bytes_accessed=4 * relative.size, transcendentals=0),
    )(relative)


def score_kernel(slot_count, half, early_ref, late_ref, message_ref, similar_hbm, gram, sem):
    width_all = early_ref.shape[0]
    transposed = (((1,), (1,)), ((), ()))
    owners, lanes = message_ref.shape
    block = width_all // 2
    copies = []
    nears, sums = [], []
    for b in range(2):
        part = slice(b * block, (b + 1) * block)
        tile = lax.dot_general(late_ref[part, :], late_ref[...], transposed, preferred_element_type=F32)
        tile += early_ref[part, :]
        gram[part, :] = tile
        copy = pltpu.make_async_copy(gram.at[part, :], similar_hbm.at[0, part, :], sem.at[b])
        copy.start()
        copies.append(copy)
        own = lax.broadcasted_iota(jnp.int32, (block, width_all), 0) + b * block
        other = lax.broadcasted_iota(jnp.int32, (block, width_all), 1)
        nears.append(jnp.max(jnp.where(own == other, 0.0, tile), axis=0, keepdims=True))
        sums.append(jnp.sum(tile, axis=0, keepdims=True))
    near = jnp.maximum(nears[0], nears[1])
    total = sums[0] + sums[1]
    square = jnp.maximum(jnp.sum(total, axis=1, keepdims=True), 0.0)
    dist = 1.0 - total * lax.rsqrt(square + 1e-06)
    slot = lax.broadcasted_iota(jnp.int32, (width_all, lanes), 0)
    within = slot - (slot // slot_count) * slot_count
    lane = lax.broadcasted_iota(jnp.int32, (width_all, lanes), 1)
    source = lax.broadcasted_iota(jnp.int32, (owners, width_all), 0) * slot_count
    member = lax.broadcasted_iota(jnp.int32, (owners, width_all), 1)
    mine = (member >= source) & (member < source + slot_count)
    out = jnp.zeros((owners, lanes), F32)
    for values, start in ((near, 0), (dist, half)):
        chosen = jnp.where(lane == within + start, 1.0, 0.0).astype(BF16)
        for piece in split3(jnp.where(mine, values, 0.0)):
            out += jnp.dot(piece, chosen, preferred_element_type=F32)
    message_ref[...] = out
    for copy in copies:
        copy.wait()


def scores(early, late, owners, slot_count, half):
    width_all = early.shape[0]
    return pl.pallas_call(
        functools.partial(score_kernel, slot_count, half),
        out_specs=(pl.BlockSpec(memory_space=pltpu.VMEM), pl.BlockSpec(memory_space=pltpu.HBM)),
        out_shape=(
            jax.ShapeDtypeStruct((owners, 2 * half), F32),
            jax.ShapeDtypeStruct((1, width_all, width_all), F32),
        ),
        scratch_shapes=[pltpu.VMEM((width_all, width_all), F32), pltpu.SemaphoreType.DMA((2,))],
        compiler_params=pltpu.CompilerParams(vmem_limit_bytes=VMEM_BYTES),
    )(early, late)


def fetch_kernel(half, message_ref, label_ref, rank_ref, valid_ref, near_ref, dist_ref):
    owners, lanes = message_ref.shape
    rows = label_ref.shape[1]
    owner = lax.broadcasted_iota(jnp.int32, (owners, rows), 0)
    chosen = jnp.where(owner == label_ref[...], 1.0, 0.0).astype(BF16)
    mine = jnp.zeros((lanes, rows), F32)
    for piece in split3(message_ref[...]):
        mine += lax.dot_general(piece, chosen, (((0,), (0,)), ((), ())), preferred_element_type=F32)
    lane = lax.broadcasted_iota(jnp.int32, (lanes, rows), 0)
    rank = rank_ref[...]
    valid = valid_ref[...].astype(F32)
    near_ref[...] = jnp.sum(jnp.where(lane == rank, mine, 0.0), axis=0) * valid
    dist_ref[...] = jnp.sum(jnp.where(lane == rank + half, mine, 0.0), axis=0) * valid


def fetch(message, label_row, rank_row, valid, half):
    rows = label_row.shape[1]
    return pl.pallas_call(
        functools.partial(fetch_kernel, half),
        out_shape=(jax.ShapeDtypeStruct((rows,), F32),) * 2,
        compiler_params=pltpu.CompilerParams(vmem_limit_bytes=FETCH_VMEM_BYTES),
    )(message, label_row, rank_row, valid)


def per_device(tokens, proj_weight, labels, valid_rows):
    row_count = tokens.shape[0]
    owners = lax.axis_size("clus")
    slot_count = 2 * row_count // owners
    width_all = owners * slot_count
    half = -(-slot_count // 64) * 64
    early = EARLY * proj_weight.shape[1] // 8
    label_row = labels.reshape(1, row_count)
    keep, send, slot_row, total, scale, rank_row = embed_and_pack(
        tokens, proj_weight, label_row, valid_rows, owners, slot_count, early
    )
    arrived = lax.all_to_all(
        pack(slot_row, total, scale, width_all, early).reshape(owners, slot_count, -1), "clus", split_axis=0, concat_axis=0, tiled=True
    )
    early_gram = order_early(spread_early(keep, send, owners, slot_count), owners, slot_count)
    message, similar = scores(early_gram, arrived.reshape(width_all, -1), owners, slot_count, half)
    returned = lax.all_to_all(message, "clus", split_axis=0, concat_axis=0, tiled=True)
    nearest, centre_dist = fetch(returned, label_row, rank_row, valid_rows, half)
    return (similar, nearest, centre_dist)


def solution(mesh):
    return jax.shard_map(
        per_device,
        mesh=mesh,
        in_specs=(
            P(("groups", "clus"), None),
            P(),
            P(("groups", "clus"), None),
            P(("groups", "clus")),
        ),
        out_specs=(P(("groups", "clus"), None, None), P(("groups", "clus")), P(("groups", "clus"))),
        check_vma=False,
    )
```
